128 devices in a mesh: ctx: 16 (over x, y), head: 8 (over z, core).
Axes of the slice: x: 4, y: 4, z: 4, core: 2. Of those that a mesh axis runs over, the one named last changes fastest.
Arguments:
- x_rows: bfloat16 [32768, 8192], P(('ctx', 'head')), may hold values from -6 to 6
- b_rows: bfloat16 [32768, 1024], P(('ctx', 'head')), may hold values from -0.5 to 0.5
- c_rows: bfloat16 [32768, 1024], P(('ctx', 'head')), may hold values from -6 to 6
- dt_rows: bfloat16 [32768, 128], P(('ctx', 'head')), may hold values from -3 to 3
- destination: int32 [256], P('ctx'), may hold values from 0 to 255, as said below
- doc_start: int32 [32768], P('ctx'), may hold values 0 or 1
- a_log: float32 [128], P('head'), may hold values from -9 to -1
- dt_bias: float32 [128], P('head'), may hold values from -8 to 0
- d_skip: float32 [128], P('head'), may hold values from 0.5 to 1.5
- cotangent: bfloat16 [32768, 8192], P('ctx', 'head'), may hold values from -6 to 6
Outputs:
- ssd_output: bfloat16 [32768, 8192], P('ctx', 'head')
- input_grad: bfloat16 [32768, 8192], P('ctx', 'head')
The draws below stay inside these ranges and needn't reach their ends.
Inputs may be any that keep to these rules, and one draw needn't show every extreme that they name: Entry p names the packed block of loader block p, and every packed block is named once. The owner of a block is destination // 16; of the 16 blocks of one loader shard at most 2 go to one owner, and in every draw some loader shard sends 2 to one owner.
All inputs are finite; a program needn't handle non-finite values. No bound on the sum of `doc_start` on one device may be relied on, other than what follows from the above.
Results may differ from the reference program's by a relative error of at most 0.004.
Values may be sent and summed in bfloat16 or wider, within the bound.
No kernel may reach another device: no remote copies, remote signals or barrier semaphores. Data moves between devices by JAX's collectives and lax.ppermute only.
A program may use at most 192 MiB of HBM per device.

```python
import jax
import jax.numpy as jnp
from jax import lax

HEADS = 128
HEAD_DIM = 64
STATE = 128
GROUPS = 8
BLOCK = 256
TOK_DEV = 2048
TOKENS = 32768
OWNERS = 16
PIECES = 256
PIECE_ROWS = 128
INNER = 8192
GROUP_STATE = 1024


def rate_pair(key, slow_share):
    first, second, third = jax.random.split(key, 3)
    slow = jax.random.uniform(first, (HEADS,), jnp.float32) < slow_share
    level = jax.random.uniform(second, (HEADS,), jnp.float32)
    slow_rate = 0.2 / TOKENS * jnp.exp(level * jnp.log(10.0))
    fast_rate = 0.02 * jnp.exp(level * jnp.log(2.5))
    rate_value = jnp.where(slow, slow_rate, fast_rate)
    factor = jax.random.uniform(third, (HEADS,), jnp.float32, 0.8, 1.2)
    step_value = jnp.sqrt(2.0 * rate_value) * factor
    return (jnp.log(rate_value / step_value), jnp.log(jnp.expm1(step_value)))


def draw_a_log(key, part):
    share = 0.5
    log_value, bias_value = rate_pair(key, share)
    return log_value.astype(jnp.float32)


def draw_dt_bias(key, part):
    share = 0.5
    log_value, bias_value = rate_pair(key, share)
    return bias_value.astype(jnp.float32)


def shuffled(subkey):
    return jax.random.permutation(subkey, OWNERS)


def draw_destination(key, part):
    key = jax.random.fold_in(key, 7)
    first, second, third = jax.random.split(key, 3)
    shift_order = jax.random.permutation(first, OWNERS)
    slot_index = jnp.arange(OWNERS, dtype=jnp.int32)
    shift_value = shift_order[slot_index * 2 // 3]
    loader = slot_index[:, None]
    owner = (loader + shift_value[None, :]) % OWNERS
    arrival = jax.vmap(shuffled)(jax.random.split(second, OWNERS))
    place = arrival[owner, slot_index[None, :]]
    order = jax.vmap(shuffled)(jax.random.split(third, OWNERS))
    packed_index = (owner * OWNERS + place).astype(jnp.int32)
    table = jnp.zeros((OWNERS, OWNERS), jnp.int32).at[loader, order].set(packed_index)
    return table.reshape(PIECES).astype(jnp.int32)


def set_ends(values, own_key, low, top_value):
    index_at = [jax.random.randint(jax.random.fold_in(own_key, axis), (), 0, length) for axis, length in enumerate(values.shape)]
    main_axis = values.shape.index(max(values.shape))
    next_to = index_at[:main_axis] + [(index_at[main_axis] + 1) % values.shape[main_axis]] + index_at[main_axis + 1:]
    return values.at[tuple(index_at)].set(low).at[tuple(next_to)].set(top_value)


def block_levels(rng, dims, cuts, smallest, largest):
    def one(axis_at, blocks):
        steps = jax.random.uniform(jax.random.fold_in(jax.random.fold_in(rng, 6), axis_at), (blocks,), jnp.float32, smallest / len(cuts), largest / len(cuts))
        return jnp.repeat(jnp.exp(steps), dims[axis_at] // blocks).reshape((-1,) + (1,) * (len(dims) - axis_at - 1))

    gain = one(*cuts[0])
    for cut in cuts[1:]:
        gain = gain * one(*cut)
    return gain


def normal_values(key, extent, scale, most, cuts=(), held_as=jnp.bfloat16):
    loudness = block_levels(key, extent, cuts, -0.22, 0.18) if cuts else 1.0
    entries = jax.random.normal(key, extent, jnp.float32) * scale * loudness
    return jnp.minimum(jnp.maximum(entries, -most), most).astype(held_as)


def setup_inputs(seed: int = 0) -> dict:
    streams_of = jax.random.split(jax.random.key(seed), 11)
    x_rows = normal_values(streams_of[0], (TOKENS, INNER), 1.0, 6.0, ((0, 128),))
    b_rows = normal_values(streams_of[1], (TOKENS, GROUP_STATE), STATE ** -0.5, 0.5, ((0, 128),))
    c_rows = normal_values(streams_of[2], (TOKENS, GROUP_STATE), 1.0, 6.0, ((0, 128),))
    dt_rows = normal_values(streams_of[3], (TOKENS, HEADS), 0.5, 3.0, ((0, 128),))
    destination = draw_destination(jax.random.fold_in(streams_of[10], 71), 0)
    doc_start = set_ends((jax.random.randint(streams_of[5], (TOKENS,), 0, 2 * TOK_DEV) < 1).astype(jnp.int32), jax.random.fold_in(streams_of[5], 1), 0, 1)
    a_log = draw_a_log(jax.random.fold_in(streams_of[10], 71), 0)
    dt_bias = draw_dt_bias(jax.random.fold_in(streams_of[10], 71), 0)
    d_skip = jnp.clip(1.0 + 0.1 * jax.random.normal(streams_of[8], (HEADS,), jnp.float32), 0.5, 1.5)
    cotangent = normal_values(streams_of[9], (TOKENS, INNER), 1.0, 6.0, ((0, 16), (1, 8)))
    return {"x_rows": x_rows, "b_rows": b_rows, "c_rows": c_rows, "dt_rows": dt_rows, "destination": destination, "doc_start": doc_start, "a_log": a_log, "dt_bias": dt_bias, "d_skip": d_skip, "cotangent": cotangent}


def rounded(value):
    return lax.optimization_barrier(value.astype(jnp.bfloat16)).astype(jnp.float32)


def block_masks(rate_blk, start_blk, b_blk, c_blk):
    block_size = rate_blk.shape[0]
    per_group = HEADS // GROUPS
    log_decay = jnp.cumsum(rate_blk, axis=0)
    segment = jnp.cumsum(start_blk)
    row_index = lax.broadcasted_iota(jnp.int32, (block_size, block_size), 0)
    col_index = lax.broadcasted_iota(jnp.int32, (block_size, block_size), 1)
    causal = (col_index <= row_index) & (segment[:, None] == segment[None, :])
    decay_rows = log_decay.T
    log_gap = decay_rows[:, :, None] - decay_rows[:, None, :]
    decay = jnp.exp(jnp.where(causal[None], log_gap, -jnp.inf))
    scores = jnp.einsum("tgs,ugs->gtu", c_blk.astype(jnp.float32), b_blk.astype(jnp.float32))
    masked = scores[:, None] * decay.reshape(GROUPS, per_group, block_size, block_size)
    entry_scale = jnp.exp(log_decay) * (segment == 0)[:, None].astype(jnp.float32)
    exit_scale = jnp.exp(log_decay[-1][None, :] - log_decay) * (segment == segment[-1])[:, None].astype(jnp.float32)
    block_decay = jnp.exp(log_decay[-1]) * (segment[-1] == 0).astype(jnp.float32)
    return masked, entry_scale, exit_scale, block_decay


def reference(x_rows, b_rows, c_rows, dt_rows, destination, doc_start, a_log, dt_bias, d_skip, cotangent):
    def packed(source):
        pieces = source.reshape(PIECES, PIECE_ROWS, source.shape[1])
        return jnp.zeros_like(pieces).at[destination].set(pieces).reshape(source.shape)

    x_pack = packed(x_rows)
    b_pack = packed(b_rows)
    c_pack = packed(c_rows)
    dt_pack = packed(dt_rows)
    step_size = jax.nn.softplus(dt_pack.astype(jnp.float32) + dt_bias)
    rate_log = -step_size * jnp.exp(a_log)
    block_count = TOKENS // BLOCK
    per_group = HEADS // GROUPS
    x_all = x_pack.reshape(block_count, BLOCK, GROUPS, per_group, HEAD_DIM)
    b_all = b_pack.reshape(block_count, BLOCK, GROUPS, STATE)
    c_all = c_pack.reshape(block_count, BLOCK, GROUPS, STATE)
    rate_all = rate_log.reshape(block_count, BLOCK, HEADS)
    step_all = step_size.reshape(block_count, BLOCK, HEADS)
    start_all = doc_start.reshape(block_count, BLOCK)
    cot_all = cotangent.reshape(block_count, BLOCK, GROUPS, per_group, HEAD_DIM)
    skip_gain = d_skip.reshape(1, GROUPS, per_group, 1)

    def forward_block(state_in, blocks):
        x_blk, b_blk, c_blk, rate_blk, step_blk, start_blk = blocks
        masked, entry_scale, exit_scale, block_decay = block_masks(rate_blk, start_blk, b_blk, c_blk)
        weights = rounded(masked * step_blk.T.reshape(GROUPS, per_group, 1, BLOCK))
        x_float = x_blk.astype(jnp.float32)
        y_diag = jnp.einsum("gjtu,ugjp->tgjp", weights, x_float)
        state_round = rounded(state_in).reshape(GROUPS, per_group, HEAD_DIM, STATE)
        y_off = jnp.einsum("tgs,gjps->tgjp", c_blk.astype(jnp.float32), state_round)
        y_off = y_off * entry_scale.reshape(BLOCK, GROUPS, per_group, 1)
        result = (y_diag + y_off + skip_gain * x_float).astype(jnp.bfloat16)
        scaled = rounded(x_float * (step_blk * exit_scale).reshape(BLOCK, GROUPS, per_group, 1))
        update = jnp.einsum("ugjp,ugs->gjps", scaled, b_blk.astype(jnp.float32)).reshape(HEADS, HEAD_DIM, STATE)
        return block_decay[:, None, None] * state_in + update, result

    def backward_block(grad_in, blocks):
        b_blk, c_blk, rate_blk, step_blk, start_blk, cot_blk = blocks
        masked, entry_scale, exit_scale, block_decay = block_masks(rate_blk, start_blk, b_blk, c_blk)
        weights = rounded(masked)
        cot_float = cot_blk.astype(jnp.float32)
        grad_diag = jnp.einsum("gjut,ugjp->tgjp", weights, cot_float)
        grad_round = rounded(grad_in).reshape(GROUPS, per_group, HEAD_DIM, STATE)
        grad_off = jnp.einsum("tgs,gjps->tgjp", b_blk.astype(jnp.float32), grad_round)
        step_four = step_blk.reshape(BLOCK, GROUPS, per_group, 1)
        step_exit = (step_blk * exit_scale).reshape(BLOCK, GROUPS, per_group, 1)
        result = (step_four * grad_diag + step_exit * grad_off + skip_gain * cot_float).astype(jnp.bfloat16)
        scaled = rounded(cot_float * entry_scale.reshape(BLOCK, GROUPS, per_group, 1))
        update = jnp.einsum("ugjp,ugs->gjps", scaled, c_blk.astype(jnp.float32)).reshape(HEADS, HEAD_DIM, STATE)
        return block_decay[:, None, None] * grad_in + update, result

    zero_state = jnp.zeros((HEADS, HEAD_DIM, STATE), jnp.float32)
    unused, outputs = lax.scan(forward_block, zero_state, (x_all, b_all, c_all, rate_all, step_all, start_all))
    unused_grad, grads = lax.scan(backward_block, zero_state, (b_all, c_all, rate_all, step_all, start_all, cot_all), reverse=True)
    return outputs.reshape(TOKENS, INNER), grads.reshape(TOKENS, INNER)
```

```python
from functools import partial

import jax
import jax.numpy as jnp
from jax import lax
from jax.experimental import pallas as pl
from jax.experimental.pallas import tpu as pltpu
from jax.sharding import PartitionSpec as P

OWNERS = 16
PEERS = 8
PIECE = 128
STATE = 128
HEADS = 16
HEAD_DIM = 64
WIDTH = HEADS * HEAD_DIM
HALF = WIDTH // 2
SMALL_ROWS = 2 * PIECE + HEADS
TAG_ROWS = 16
SENT_ROWS = SMALL_ROWS + TAG_ROWS
EXTRA = 128
LOG2E = 1.4426950408889634
F32 = jnp.float32
BF16 = jnp.bfloat16
ANY = pl.BlockSpec(memory_space=pltpu.HBM)
SMEM = pl.BlockSpec(memory_space=pltpu.SMEM)
SHIFTS = [(1, 0), (3, 0), (1, 1), (3, 1), (2, 0), (2, 1), (0, 1)]


def params(mib=48):
    return pltpu.CompilerParams(vmem_limit_bytes=mib * 1024 * 1024)


def partner(head, shift):
    return (head // 2 + shift[0]) % 4 * 2 + (head % 2 + shift[1]) % 2


def source(head, shift):
    return (head // 2 + 4 - shift[0]) % 4 * 2 + (head % 2 + shift[1]) % 2


def run_copies(copies):
    for copy in copies:
        copy.start()
    for copy in copies:
        copy.wait()


def gather_small_kernel(b_ref, c_ref, dt_ref, out_ref, turned, sems):
    copies = []
    for r in range(2):
        rows = pl.ds(r * PIECE, PIECE)
        for g in range(PEERS):
            cols = pl.ds(g * STATE, STATE)
            for kind, ref in enumerate((b_ref, c_ref)):
                copies.append(
                    pltpu.make_async_copy(
                        ref.at[rows, cols],
                        out_ref.at[g, r, pl.ds(kind * PIECE, PIECE), :],
                        sems.at[len(copies)],
                    )
                )
    for copy in copies:
        copy.start()
    last = []
    for r in range(2):
        dt_t = dt_ref[r * PIECE : (r + 1) * PIECE, :].astype(F32).T.astype(BF16)
        for g in range(PEERS):
            turned[g, r] = dt_t[g * HEADS : (g + 1) * HEADS, :]
    last = pltpu.make_async_copy(
        turned, out_ref.at[:, :, pl.ds(2 * PIECE, HEADS), :], sems.at[len(copies)]
    )
    last.start()
    for copy in copies + [last]:
        copy.wait()


def gather_small(b_rows, c_rows, dt_rows):
    return pl.pallas_call(
        gather_small_kernel,
        in_specs=[ANY, ANY, pl.BlockSpec(memory_space=pltpu.VMEM)],
        out_specs=ANY,
        out_shape=jax.ShapeDtypeStruct((PEERS, 2, SMALL_ROWS, STATE), BF16),
        scratch_shapes=[
            pltpu.VMEM((PEERS, 2, HEADS, PIECE), BF16),
            pltpu.SemaphoreType.DMA((4 * PEERS + 1,)),
        ],
        compiler_params=params(),
        name="gather_small",
    )(b_rows, c_rows, dt_rows)


def pack_small_kernel(slot_ref, place_ref, in_ref, out_ref, tags, sems):
    copies = [
        pltpu.make_async_copy(
            in_ref.at[j], out_ref.at[slot_ref[j], pl.ds(0, SMALL_ROWS), :], sems.at[j]
        )
        for j in range(OWNERS)
    ]
    for copy in copies:
        copy.start()
    tags[...] = jnp.full(tags.shape, -1.0, BF16)
    for j in range(OWNERS):
        place = place_ref[j].astype(F32)
        tags[slot_ref[j]] = jnp.full(tags.shape[1:], place, F32).astype(BF16)
    last = pltpu.make_async_copy(
        tags, out_ref.at[:, pl.ds(SMALL_ROWS, TAG_ROWS), :], sems.at[OWNERS]
    )
    last.start()
    for copy in copies + [last]:
        copy.wait()


def pack_small(slot, place, pieces):
    return pl.pallas_call(
        pack_small_kernel,
        in_specs=[SMEM, SMEM, ANY],
        out_specs=ANY,
        out_shape=jax.ShapeDtypeStruct((2 * OWNERS, SENT_ROWS, STATE), BF16),
        scratch_shapes=[
            pltpu.VMEM((2 * OWNERS, TAG_ROWS, STATE), BF16),
            pltpu.SemaphoreType.DMA((OWNERS + 1,)),
        ],
        compiler_params=params(),
        name="pack_small",
    )(slot, place, pieces)


def find_source_kernel(small_ref, out_ref, tags, sem):
    copy = pltpu.make_async_copy(
        small_ref.at[:, pl.ds(SMALL_ROWS, TAG_ROWS), :], tags, sem.at[0]
    )
    copy.start()
    copy.wait()
    slot = lax.broadcasted_iota(jnp.int32, tags.shape, 0).astype(F32)
    place = lax.broadcasted_iota(jnp.int32, tags.shape, 2).astype(F32)
    found = jnp.where(tags[...].astype(F32) == place, slot, 0.0)
    out_ref[...] = jnp.sum(found, axis=0)[0:1].astype(jnp.int32)


def find_source(small):
    return pl.pallas_call(
        find_source_kernel,
        in_specs=[ANY],
        out_specs=pl.BlockSpec(memory_space=pltpu.VMEM),
        out_shape=jax.ShapeDtypeStruct((1, STATE), jnp.int32),
        scratch_shapes=[
            pltpu.VMEM((2 * OWNERS, TAG_ROWS, STATE), BF16),
            pltpu.SemaphoreType.DMA((1,)),
        ],
        compiler_params=params(),
        name="find_source",
    )(small)


def cut_kernel(half, dest_ref, x_ref, *rest):
    outs, sems = rest[:-1], rest[-1]
    copies = []
    for i, out_ref in enumerate(outs):
        at = pl.multiple_of(dest_ref[i] * WIDTH + half * HALF, HALF)
        copies.append(pltpu.make_async_copy(x_ref.at[:, pl.ds(at, HALF)], out_ref, sems.at[i]))
    for copy in copies:
        copy.start()
    for copy in copies:
        copy.wait()


def cut(half, dest, x_rows):
    count = len(SHIFTS)
    return pl.pallas_call(
        partial(cut_kernel, half),
        in_specs=[SMEM, ANY],
        out_specs=[ANY] * count,
        out_shape=[jax.ShapeDtypeStruct((x_rows.shape[0], HALF), BF16)] * count,
        scratch_shapes=[pltpu.SemaphoreType.DMA((count,))],
        compiler_params=params(),
        name="cut",
    )(dest, x_rows)


def pack_x_kernel(half, slot_ref, from_ref, x_ref, *rest):
    arrived, out_ref, sems = rest[:-2], rest[-2], rest[-1]
    count = len(arrived)
    at = pl.multiple_of(from_ref[count] * WIDTH + half * HALF, HALF)
    copies = []
    for i in range(count + 1):
        for r in range(2):
            slot = slot_ref[from_ref[i] * 2 + r]
            rows = pl.ds(r * PIECE, PIECE)
            piece = arrived[i].at[rows, :] if i < count else x_ref.at[rows, pl.ds(at, HALF)]
            copies.append(pltpu.make_async_copy(piece, out_ref.at[slot], sems.at[2 * i + r]))
    for copy in copies:
        copy.start()
    for copy in copies:
        copy.wait()


def pack_x(half, slot, origin, x_rows, arrived):
    return pl.pallas_call(
        partial(pack_x_kernel, half),
        in_specs=[SMEM, SMEM] + [ANY] * (1 + len(arrived)),
        out_specs=ANY,
        out_shape=jax.ShapeDtypeStruct((2 * OWNERS, PIECE, HALF), BF16),
        scratch_shapes=[pltpu.SemaphoreType.DMA((2 * PEERS,))],
        compiler_params=params(),
        name="pack_x",
    )(slot, origin, x_rows, *arrived)


def split_two(value):
    high = value.astype(BF16)
    return high, (value - high.astype(F32)).astype(BF16)


def softplus(value):
    small = jnp.exp(-jnp.abs(value))
    series = small * (1.0 - small * (0.5 - small * (1.0 / 3.0 - small * 0.25)))
    return jnp.maximum(value, 0.0) + jnp.where(small < 1e-2, series, jnp.log(1.0 + small))


def decay_kernel(
    src_ref, small_ref, seg_ref, bias_ref, alog_ref, rows_ref, scale_ref, ends_ref, total_ref, dt_ref, sems
):
    pieces = seg_ref.shape[0]
    copies = [
        pltpu.make_async_copy(
            small_ref.at[src_ref[0, k], pl.ds(2 * PIECE, HEADS), :], dt_ref.at[k], sems.at[k]
        )
        for k in range(pieces)
    ]
    for copy in copies:
        copy.start()
    for copy in copies:
        copy.wait()
    step_all = softplus(dt_ref[...].astype(F32) + bias_ref[...][None])
    rate_all = -step_all * (jnp.exp(alog_ref[...]) * LOG2E)[None]
    up_to = (
        lax.broadcasted_iota(jnp.int32, (PIECE, PIECE), 0)
        <= lax.broadcasted_iota(jnp.int32, (PIECE, PIECE), 1)
    ).astype(F32)
    log_all = jnp.dot(
        rate_all.reshape(pieces * HEADS, PIECE),
        up_to,
        precision=lax.Precision.HIGHEST,
        preferred_element_type=F32,
    ).reshape(pieces, HEADS, PIECE)
    ends = [log_all[k, :, PIECE - 1 :] for k in range(pieces)]
    starts = [seg_ref[k, :, PIECE - 1 :] for k in range(pieces)]
    log_before = jnp.zeros((HEADS, 1), F32)
    starts_before = jnp.zeros((1, 1), F32)
    rows_ref[...] = jnp.zeros(rows_ref.shape, F32)
    for k in range(pieces):
        log, step, seg = log_all[k], step_all[k], seg_ref[k]
        rows_ref[k, 0:HEADS, :] = log
        rows_ref[k, HEADS : 2 * HEADS, :] = log - jnp.log(step) * LOG2E
        rows_ref[k, 2 * HEADS : 2 * HEADS + 1, :] = seg
        none_yet = (seg == 0.0).astype(F32)
        none_left = (seg == starts[k]).astype(F32)
        entry = jnp.exp2(log) * none_yet
        step_exit = step * (jnp.exp2(ends[k] - log) * none_left)
        decay = jnp.exp2(ends[k]) * (starts[k] == 0.0).astype(F32)
        before = jnp.exp2(log_before + log) * (none_yet * (starts_before == 0.0).astype(F32))
        for at, value in enumerate(
            (entry, step_exit, step, jnp.broadcast_to(decay, entry.shape))
        ):
            high, low = split_two(value)
            scale_ref[k, 2 * at * HEADS : (2 * at + 1) * HEADS, :] = high
            scale_ref[k, (2 * at + 1) * HEADS : (2 * at + 2) * HEADS, :] = low
        high, low = split_two(before)
        ends_ref[k, 0:HEADS, :] = high
        ends_ref[k, HEADS : 2 * HEADS, :] = low
        log_before = log_before + ends[k]
        starts_before = starts_before + starts[k]
    total_ref[...] = jnp.broadcast_to(
        jnp.exp2(log_before) * (starts_before == 0.0).astype(F32), total_ref.shape
    )
    log_after = jnp.zeros((HEADS, 1), F32)
    starts_after = jnp.zeros((1, 1), F32)
    for k in reversed(range(pieces)):
        log, step, seg = log_all[k], step_all[k], seg_ref[k]
        none_left = (seg == starts[k]).astype(F32) * (starts_after == 0.0).astype(F32)
        after = step * (jnp.exp2(log_after + (ends[k] - log)) * none_left)
        high, low = split_two(after)
        ends_ref[k, 2 * HEADS : 3 * HEADS, :] = high
        ends_ref[k, 3 * HEADS : 4 * HEADS, :] = low
        log_after = log_after + ends[k]
        starts_after = starts_after + starts[k]


ROW_COUNT = 40


def decays(src, small, seg, bias, alog):
    pieces = seg.shape[0]
    whole = pl.BlockSpec(memory_space=pltpu.VMEM)
    return pl.pallas_call(
        decay_kernel,
        in_specs=[SMEM, ANY, whole, whole, whole],
        out_specs=[whole] * 4,
        out_shape=[
            jax.ShapeDtypeStruct((pieces, ROW_COUNT, PIECE), F32),
            jax.ShapeDtypeStruct((pieces, 8 * HEADS, PIECE), BF16),
            jax.ShapeDtypeStruct((pieces, 4 * HEADS, PIECE), BF16),
            jax.ShapeDtypeStruct((HEADS, PIECE), F32),
        ],
        scratch_shapes=[
            pltpu.VMEM((pieces, HEADS, PIECE), BF16),
            pltpu.SemaphoreType.DMA((pieces,)),
        ],
        compiler_params=params(),
        name="decays",
    )(src, small, seg, bias, alog)


def spread(kinds):
    rows = lax.broadcasted_iota(jnp.int32, (kinds, kinds * 2 * HEADS, WIDTH), 1)
    kind = lax.broadcasted_iota(jnp.int32, (kinds, kinds * 2 * HEADS, WIDTH), 0)
    head = lax.broadcasted_iota(jnp.int32, (kinds, kinds * 2 * HEADS, WIDTH), 2) // HEAD_DIM
    return ((rows // (2 * HEADS) == kind) & (rows % HEADS == head)).astype(BF16)


def over_first(left, right):
    return lax.dot_general(left, right, (((0,), (0,)), ((), ())), preferred_element_type=F32)


def over_last(left, right):
    return lax.dot_general(left, right, (((1,), (1,)), ((), ())), preferred_element_type=F32)


def two_heads(weights, values):
    lane = lax.broadcasted_iota(jnp.int32, values.shape, 1)
    zero = jnp.zeros_like(values)
    stacked = jnp.concatenate(
        [jnp.where(lane < HEAD_DIM, values, zero), jnp.where(lane < HEAD_DIM, zero, values)], axis=0
    )
    return jnp.dot(jnp.concatenate(weights, axis=1), stacked, preferred_element_type=F32)


ENTRY, STEP_EXIT, STEP, DECAY = range(4)


def forward_kernel(
    first, src_ref, small_ref, x_ref, rows_ref, scale_ref, spread_ref, skip_ref, y_ref, out_ref, state
):
    step = pl.program_id(0)

    @pl.when(step == 0)
    def _():
        state[...] = jnp.zeros_like(state)

    b, c = small_ref[0, 0:PIECE, :], small_ref[0, PIECE : 2 * PIECE, :]
    scales = scale_ref[0]
    by_token = rows_ref[0].T
    row = lax.broadcasted_iota(jnp.int32, (PIECE, PIECE), 0)
    col = lax.broadcasted_iota(jnp.int32, (PIECE, PIECE), 1)
    same = by_token[:, 2 * HEADS : 2 * HEADS + 1] == rows_ref[0, 2 * HEADS : 2 * HEADS + 1, :]
    scores = jnp.where((col <= row) & same, over_last(c, b), 0.0)
    for pair in range(x_ref.shape[2] // (2 * HEAD_DIM)):
        cols = slice(pair * 2 * HEAD_DIM, (pair + 1) * 2 * HEAD_DIM)
        weights = []
        for head in (first + 2 * pair, first + 2 * pair + 1):
            gap = by_token[:, head : head + 1] - rows_ref[0, HEADS + head : HEADS + head + 1, :]
            weights.append((scores * jnp.exp2(jnp.minimum(gap, 8.0))).astype(BF16))
        x = x_ref[0, :, cols]
        x_wide = x.astype(F32)
        held = state[:, cols]
        y = two_heads(weights, x) + skip_ref[:, cols] * x_wide
        y += over_first(scales, spread_ref[ENTRY, :, cols]) * jnp.dot(
            c, held.astype(BF16), preferred_element_type=F32
        )
        y_ref[0, :, cols] = y
        x_scaled = (x_wide * over_first(scales, spread_ref[STEP_EXIT, :, cols])).astype(BF16)
        state[:, cols] = over_first(scales, spread_ref[DECAY, :, cols]) * held + over_first(b, x_scaled)

    @pl.when(step == pl.num_programs(0) - 1)
    def _():
        out_ref[...] = state[...].astype(BF16)


def forward_local(half, src, small, x_slots, rows, scales, spread_four, skip):
    pieces = rows.shape[0]
    return pl.pallas_call(
        partial(forward_kernel, half * HEADS // 2),
        grid_spec=pltpu.PrefetchScalarGridSpec(
            num_scalar_prefetch=1,
            grid=(pieces,),
            in_specs=[
                pl.BlockSpec((1, 2 * PIECE, STATE), lambda k, src: (src[0, k], 0, 0)),
                pl.BlockSpec((1, PIECE, HALF), lambda k, src: (src[0, k], 0, 0)),
                pl.BlockSpec((1, ROW_COUNT, PIECE), lambda k, src: (k, 0, 0)),
                pl.BlockSpec((1, 8 * HEADS, PIECE), lambda k, src: (k, 0, 0)),
                pl.BlockSpec((4, 8 * HEADS, HALF), lambda k, src: (0, 0, half)),
                pl.BlockSpec((1, HALF), lambda k, src: (0, half)),
            ],
            out_specs=[
                pl.BlockSpec((1, PIECE, HALF), lambda k, src: (k, 0, 0)),
                pl.BlockSpec((STATE, HALF), lambda k, src: (0, 0)),
            ],
            scratch_shapes=[pltpu.VMEM((STATE, HALF), F32)],
        ),
        out_shape=[
            jax.ShapeDtypeStruct((pieces, PIECE, HALF), F32),
            jax.ShapeDtypeStruct((STATE, HALF), BF16),
        ],
        compiler_params=params(),
        name="forward_local",
    )(src, small, x_slots, rows, scales, spread_four, skip)


def forward_state_kernel(half, src_ref, small_ref, x_ref, ends_ref, spread_ref, out_ref, b_all, x_all, state, sems):
    pieces = ends_ref.shape[0]
    copies = []
    for k in range(pieces):
        at = src_ref[0, k]
        copies.append(
            (
                pltpu.make_async_copy(small_ref.at[at, pl.ds(0, PIECE), :], b_all.at[k], sems.at[2 * k]),
                pltpu.make_async_copy(x_ref.at[at], x_all.at[k], sems.at[2 * k + 1]),
            )
        )
    for pair in copies:
        for copy in pair:
            copy.start()
    for k, pair in enumerate(copies):
        for copy in pair:
            copy.wait()
        after = over_first(ends_ref[k], spread_ref[1, :, half * HALF : (half + 1) * HALF])
        x_scaled = (x_all[k].astype(F32) * after).astype(BF16)
        update = over_first(b_all[k], x_scaled)
        state[...] = update if k == 0 else state[...] + update
    out_ref[...] = state[...].astype(BF16)


def forward_state(half, src, small, x_slots, ends, spread_two):
    whole = pl.BlockSpec(memory_space=pltpu.VMEM)
    pieces = ends.shape[0]
    return pl.pallas_call(
        partial(forward_state_kernel, half),
        in_specs=[SMEM, ANY, ANY, whole, whole],
        out_specs=whole,
        out_shape=jax.ShapeDtypeStruct((STATE, HALF), BF16),
        scratch_shapes=[
            pltpu.VMEM((pieces, PIECE, STATE), BF16),
            pltpu.VMEM((pieces, PIECE, HALF), BF16),
            pltpu.VMEM((STATE, HALF), F32),
            pltpu.SemaphoreType.DMA((2 * pieces,)),
        ],
        compiler_params=params(),
        name="forward_state",
    )(src, small, x_slots, ends, spread_two)


def backward_kernel(
    src_ref, small_ref, cot_ref, rows_ref, scale_ref, spread_ref, skip_ref, g_ref, out_ref, state
):
    step = pl.program_id(0)

    @pl.when(step == 0)
    def _():
        state[...] = jnp.zeros_like(state)

    b, c = small_ref[0, 0:PIECE, :], small_ref[0, PIECE : 2 * PIECE, :]
    scales = scale_ref[0]
    by_token = rows_ref[0].T
    row = lax.broadcasted_iota(jnp.int32, (PIECE, PIECE), 0)
    col = lax.broadcasted_iota(jnp.int32, (PIECE, PIECE), 1)
    same = by_token[:, 2 * HEADS : 2 * HEADS + 1] == rows_ref[0, 2 * HEADS : 2 * HEADS + 1, :]
    scores = jnp.where((col >= row) & same, over_last(b, c), 0.0)
    for pair in range(HEADS // 2):
        cols = slice(pair * 2 * HEAD_DIM, (pair + 1) * 2 * HEAD_DIM)
        weights = []
        for head in (2 * pair, 2 * pair + 1):
            gap = rows_ref[0, head : head + 1, :] - by_token[:, head : head + 1]
            weights.append((scores * jnp.exp2(jnp.minimum(gap, 1.0))).astype(BF16))
        cot = cot_ref[:, cols]
        cot_wide = cot.astype(F32)
        held = state[:, cols]
        g = over_first(scales, spread_ref[STEP, :, cols]) * two_heads(weights, cot)
        g += skip_ref[:, cols] * cot_wide
        g += over_first(scales, spread_ref[STEP_EXIT, :, cols]) * jnp.dot(
            b, held.astype(BF16), preferred_element_type=F32
        )
        g_ref[0, :, cols] = g
        cot_scaled = (cot_wide * over_first(scales, spread_ref[ENTRY, :, cols])).astype(BF16)
        state[:, cols] = over_first(scales, spread_ref[DECAY, :, cols]) * held + over_first(c, cot_scaled)

    @pl.when(step == pl.num_programs(0) - 1)
    def _():
        out_ref[...] = state[...].astype(BF16)


def backward_local(src, small, cotangent, rows, scales, spread_four, skip):
    pieces = rows.shape[0]
    last = pieces - 1
    return pl.pallas_call(
        backward_kernel,
        grid_spec=pltpu.PrefetchScalarGridSpec(
            num_scalar_prefetch=1,
            grid=(pieces,),
            in_specs=[
                pl.BlockSpec((1, 2 * PIECE, STATE), lambda k, src: (src[0, last - k], 0, 0)),
                pl.BlockSpec((PIECE, WIDTH), lambda k, src: (last - k, 0)),
                pl.BlockSpec((1, ROW_COUNT, PIECE), lambda k, src: (last - k, 0, 0)),
                pl.BlockSpec((1, 8 * HEADS, PIECE), lambda k, src: (last - k, 0, 0)),
                pl.BlockSpec((4, 8 * HEADS, WIDTH), lambda k, src: (0, 0, 0)),
                pl.BlockSpec((1, WIDTH), lambda k, src: (0, 0)),
            ],
            out_specs=[
                pl.BlockSpec((1, PIECE, WIDTH), lambda k, src: (last - k, 0, 0)),
                pl.BlockSpec((STATE, WIDTH), lambda k, src: (0, 0)),
            ],
            scratch_shapes=[pltpu.VMEM((STATE, WIDTH), F32)],
        ),
        out_shape=[
            jax.ShapeDtypeStruct((pieces, PIECE, WIDTH), F32),
            jax.ShapeDtypeStruct((STATE, WIDTH), BF16),
        ],
        compiler_params=params(),
        name="backward_local",
    )(src, small, cotangent, rows, scales, spread_four, skip)


def join_kernel(a_ref, b_ref, g_ref, total_ref, out_ref):
    high, low = split_two(total_ref[...])
    lane = lax.broadcasted_iota(jnp.int32, high.shape, 1)
    decay = jnp.where(lane == 0, high, jnp.where(lane == 1, low, jnp.zeros_like(low)))
    for part in range(OWNERS):
        rows = slice(part % 8 * 16, part % 8 * 16 + 16)
        if part < 8:
            out_ref[part, :, 0:HALF] = a_ref[rows, :]
            out_ref[part, :, HALF:WIDTH] = b_ref[rows, :]
        else:
            out_ref[part, :, 0:WIDTH] = g_ref[rows, :]
        out_ref[part, :, WIDTH:] = decay


def join_states(state_a, state_b, g_state, total):
    return pl.pallas_call(
        join_kernel,
        out_shape=jax.ShapeDtypeStruct((OWNERS, 16, WIDTH + EXTRA), BF16),
        compiler_params=params(),
        name="join_states",
    )(state_a, state_b, g_state, total)


def scan_kernel(back_ref, part_ref, out_ref):
    back = back_ref[0]
    head = lax.broadcasted_iota(jnp.int32, (HEADS, WIDTH), 0)
    lane = lax.broadcasted_iota(jnp.int32, (HEADS, WIDTH), 1)
    spread_one = (lane // HEAD_DIM == head).astype(BF16)

    def hop(k, held):
        at = jnp.where(back == 1, OWNERS - 1 - k, k)
        out_ref[at] = held.astype(BF16)
        decay = over_first(part_ref[at, :, WIDTH:], spread_one)
        return (decay[0:1] + decay[1:2]) * held + part_ref[at, :, 0:WIDTH].astype(F32)

    lax.fori_loop(0, OWNERS, hop, jnp.zeros((HEADS, WIDTH), F32), unroll=4)


def scan_owners(back, parts):
    whole = pl.BlockSpec(memory_space=pltpu.VMEM)
    return pl.pallas_call(
        scan_kernel,
        in_specs=[SMEM, whole],
        out_specs=whole,
        out_shape=jax.ShapeDtypeStruct((OWNERS, 16, WIDTH), BF16),
        compiler_params=params(),
        name="scan_owners",
    )(back, parts)


def finish_kernel(
    src_ref, small_ref, ya_ref, yb_ref, g_ref, enter_ref, ends_ref, spread_ref, y_out, g_out
):
    b, c = small_ref[0, 0:PIECE, :], small_ref[0, PIECE : 2 * PIECE, :]
    ends = ends_ref[0]
    for half, y_ref in enumerate((ya_ref, yb_ref)):
        cols = slice(half * HALF, (half + 1) * HALF)
        y_off = jnp.dot(c, enter_ref[0:STATE, cols], preferred_element_type=F32)
        y = y_ref[0] + over_first(ends, spread_ref[0, :, cols]) * y_off
        y_out[:, cols] = y.astype(BF16)
        g_off = jnp.dot(b, enter_ref[STATE:, cols], preferred_element_type=F32)
        g = g_ref[0, :, cols] + over_first(ends, spread_ref[1, :, cols]) * g_off
        g_out[:, cols] = g.astype(BF16)


def finish(src, small, y_a, y_b, g_local, enter, ends, spread_two):
    pieces = ends.shape[0]
    out = jax.ShapeDtypeStruct((pieces * PIECE, WIDTH), BF16)
    return pl.pallas_call(
        finish_kernel,
        grid_spec=pltpu.PrefetchScalarGridSpec(
            num_scalar_prefetch=1,
            grid=(pieces,),
            in_specs=[
                pl.BlockSpec((1, 2 * PIECE, STATE), lambda k, src: (src[0, k], 0, 0)),
                pl.BlockSpec((1, PIECE, HALF), lambda k, src: (k, 0, 0)),
                pl.BlockSpec((1, PIECE, HALF), lambda k, src: (k, 0, 0)),
                pl.BlockSpec((1, PIECE, WIDTH), lambda k, src: (k, 0, 0)),
                pl.BlockSpec((2 * STATE, WIDTH), lambda k, src: (0, 0)),
                pl.BlockSpec((1, 4 * HEADS, PIECE), lambda k, src: (k, 0, 0)),
                pl.BlockSpec((2, 4 * HEADS, WIDTH), lambda k, src: (0, 0, 0)),
            ],
            out_specs=[pl.BlockSpec((PIECE, WIDTH), lambda k, src: (k, 0))] * 2,
        ),
        out_shape=[out, out],
        compiler_params=params(),
        name="finish",
    )(src, small, y_a, y_b, g_local, enter, ends, spread_two)


def ranks(dest):
    owner = dest // OWNERS
    here = lax.broadcasted_iota(jnp.int32, (OWNERS, OWNERS), 0)
    other = lax.broadcasted_iota(jnp.int32, (OWNERS, OWNERS), 1)
    same = (owner[..., None, :] == owner[..., :, None]) & (other < here)
    return jnp.sum(same.astype(jnp.int32), axis=-1)


def to_owners(value):
    return lax.all_to_all(value, "ctx", split_axis=0, concat_axis=0, tiled=True)


def body(
    x_rows, b_rows, c_rows, dt_rows, destination, doc_start, a_log, dt_bias, d_skip, cotangent
):
    head = lax.axis_index("head")
    me = lax.axis_index("ctx")
    dest_heads = jnp.stack([partner(head, s) for s in SHIFTS]).astype(jnp.int32)
    origin = jnp.stack([source(head, s) for s in SHIFTS] + [head]).astype(jnp.int32)
    send_slot = destination // OWNERS * 2 + ranks(destination)

    small = gather_small(b_rows, c_rows, dt_rows)
    small = lax.all_to_all(small, "head", split_axis=0, concat_axis=0, tiled=True)
    small = small.reshape(OWNERS, SMALL_ROWS, STATE)
    small = to_owners(pack_small(send_slot, destination % OWNERS, small))
    src = find_source(small)

    x_slots = []
    for half in range(2):
        arrived = []
        for shift, piece in zip(SHIFTS, cut(half, dest_heads, x_rows)):
            pairs = [(h, partner(h, shift)) for h in range(PEERS)]
            arrived.append(lax.ppermute(piece, "head", pairs))
        x_slots.append(to_owners(pack_x(half, send_slot, origin, x_rows, arrived)))

    pieces = destination.shape[0]
    seg = jnp.cumsum(doc_start.reshape(pieces, PIECE), axis=1).astype(F32)[:, None, :]
    rows, scales, ends, total = decays(
        src, small, seg, dt_bias.reshape(HEADS, 1), a_log.reshape(HEADS, 1)
    )
    skip = jnp.repeat(d_skip, HEAD_DIM).reshape(1, WIDTH)
    spread_four, spread_two = spread(4), spread(2)

    g_local, g_state = backward_local(src, small, cotangent, rows, scales, spread_four, skip)
    y_a, state_a = forward_local(0, src, small, x_slots[0], rows, scales, spread_four, skip)
    state_b = forward_state(1, src, small, x_slots[1], ends, spread_two)
    y_b, unused = forward_local(1, src, small, x_slots[1], rows, scales, spread_four, skip)

    parts = to_owners(join_states(state_a, state_b, g_state, total))
    back = (me >= OWNERS // 2).astype(jnp.int32).reshape(1)
    enter = to_owners(scan_owners(back, parts)).reshape(2 * STATE, WIDTH)
    y, g = finish(src, small, y_a, y_b, g_local, enter, ends, spread_two)
    return (y, g)


def solution(mesh):
    in_specs = (
        P(("ctx", "head"), None),
        P(("ctx", "head"), None),
        P(("ctx", "head"), None),
        P(("ctx", "head"), None),
        P("ctx"),
        P("ctx"),
        P("head"),
        P("head"),
        P("head"),
        P("ctx", "head"),
    )
    out_specs = (P("ctx", "head"), P("ctx", "head"))
    return jax.shard_map(body, mesh=mesh, in_specs=in_specs, out_specs=out_specs, check_vma=False)
```

```python
from functools import partial

import jax
import jax.numpy as jnp
from jax import lax
from jax.experimental import pallas as pl
from jax.experimental.pallas import tpu as pltpu
from jax.sharding import PartitionSpec as P

OWNERS = 16
PEERS = 8
PIECE = 128
STATE = 128
HEADS = 16
HEAD_DIM = 64
WIDTH = HEADS * HEAD_DIM
HALF = WIDTH // 2
SMALL_ROWS = 2 * PIECE + HEADS
TAG_ROWS = 16
SENT_ROWS = SMALL_ROWS + TAG_ROWS
EXTRA = 128
LOG2E = 1.4426950408889634
F32 = jnp.float32
BF16 = jnp.bfloat16
ANY = pl.BlockSpec(memory_space=pl.ANY)
WHOLE = pl.BlockSpec(memory_space=pltpu.VMEM)
SMEM = pl.BlockSpec(memory_space=pltpu.SMEM)
SHIFTS = [(1, 0), (3, 0), (1, 1), (3, 1), (2, 0), (2, 1), (0, 1)]


def params(mib=56):
    return pltpu.CompilerParams(vmem_limit_bytes=mib * 1024 * 1024)


def partner(head, shift):
    return (head // 2 + shift[0]) % 4 * 2 + (head % 2 + shift[1]) % 2


def source(head, shift):
    return (head // 2 + 4 - shift[0]) % 4 * 2 + (head % 2 + shift[1]) % 2


def run_copies(copies):
    for copy in copies:
        copy.start()
    for copy in copies:
        copy.wait()


def gather_small_kernel(b_ref, c_ref, dt_ref, out_ref, turned, sems):
    copies = []
    for r in range(2):
        rows = pl.ds(r * PIECE, PIECE)
        for g in range(PEERS):
            cols = pl.ds(g * STATE, STATE)
            for kind, ref in enumerate((b_ref, c_ref)):
                copies.append(
                    pltpu.make_async_copy(
                        ref.at[rows, cols],
                        out_ref.at[g, r, pl.ds(kind * PIECE, PIECE), :],
                        sems.at[len(copies)],
                    )
                )
    for copy in copies:
        copy.start()
    last = []
    for r in range(2):
        dt_t = dt_ref[r * PIECE : (r + 1) * PIECE, :].astype(F32).T.astype(BF16)
        for g in range(PEERS):
            turned[g, r] = dt_t[g * HEADS : (g + 1) * HEADS, :]
    last = pltpu.make_async_copy(
        turned, out_ref.at[:, :, pl.ds(2 * PIECE, HEADS), :], sems.at[len(copies)]
    )
    last.start()
    for copy in copies + [last]:
        copy.wait()


def gather_small(b_rows, c_rows, dt_rows):
    return pl.pallas_call(
        gather_small_kernel,
        in_specs=[WHOLE, WHOLE, WHOLE],
        out_specs=ANY,
        out_shape=jax.ShapeDtypeStruct((PEERS, 2, SMALL_ROWS, STATE), BF16),
        scratch_shapes=[
            pltpu.VMEM((PEERS, 2, HEADS, PIECE), BF16),
            pltpu.SemaphoreType.DMA((4 * PEERS + 1,)),
        ],
        compiler_params=params(),
        name="gather_small",
    )(b_rows, c_rows, dt_rows)


def pack_small_kernel(slot_ref, place_ref, in_ref, out_ref, tags, sems):
    copies = [
        pltpu.make_async_copy(
            in_ref.at[j], out_ref.at[slot_ref[j], pl.ds(0, SMALL_ROWS), :], sems.at[j]
        )
        for j in range(OWNERS)
    ]
    for copy in copies:
        copy.start()
    tags[...] = jnp.full(tags.shape, -1.0, BF16)
    for j in range(OWNERS):
        place = place_ref[j].astype(F32)
        tags[slot_ref[j]] = jnp.full(tags.shape[1:], place, F32).astype(BF16)
    last = pltpu.make_async_copy(
        tags, out_ref.at[:, pl.ds(SMALL_ROWS, TAG_ROWS), :], sems.at[OWNERS]
    )
    last.start()
    for copy in copies + [last]:
        copy.wait()


def pack_small(slot, place, pieces):
    return pl.pallas_call(
        pack_small_kernel,
        in_specs=[SMEM, SMEM, WHOLE],
        out_specs=ANY,
        out_shape=jax.ShapeDtypeStruct((2 * OWNERS, SENT_ROWS, STATE), BF16),
        scratch_shapes=[
            pltpu.VMEM((2 * OWNERS, TAG_ROWS, STATE), BF16),
            pltpu.SemaphoreType.DMA((OWNERS + 1,)),
        ],
        compiler_params=params(),
        name="pack_small",
    )(slot, place, pieces)


def find_source_kernel(small_ref, out_ref, tags, sem):
    copy = pltpu.make_async_copy(
        small_ref.at[:, pl.ds(SMALL_ROWS, TAG_ROWS), :], tags, sem.at[0]
    )
    copy.start()
    copy.wait()
    slot = lax.broadcasted_iota(jnp.int32, tags.shape, 0).astype(F32)
    place = lax.broadcasted_iota(jnp.int32, tags.shape, 2).astype(F32)
    found = jnp.where(tags[...].astype(F32) == place, slot, 0.0)
    out_ref[...] = jnp.sum(found, axis=0)[0:1].astype(jnp.int32)


def find_source(small):
    return pl.pallas_call(
        find_source_kernel,
        in_specs=[ANY],
        out_specs=pl.BlockSpec(memory_space=pltpu.VMEM),
        out_shape=jax.ShapeDtypeStruct((1, STATE), jnp.int32),
        scratch_shapes=[
            pltpu.VMEM((2 * OWNERS, TAG_ROWS, STATE), BF16),
            pltpu.SemaphoreType.DMA((1,)),
        ],
        compiler_params=params(),
        name="find_source",
    )(small)


def cut_kernel(half, dest_ref, x_ref, *rest):
    count = len(SHIFTS)
    outs, (held, sems) = rest[:count], rest[count:]
    ins, copies = [], []
    for i in range(count):
        at = pl.multiple_of(dest_ref[i] * WIDTH + half * HALF, HALF)
        ins.append(pltpu.make_async_copy(x_ref.at[:, pl.ds(at, HALF)], held.at[i], sems.at[0, i]))
        copies.append(pltpu.make_async_copy(held.at[i], outs[i], sems.at[1, i]))
    for copy in ins:
        copy.start()
    for i in range(count):
        ins[i].wait()
        copies[i].start()
    for copy in copies:
        copy.wait()


def cut(half, dest, x_rows):
    count = len(SHIFTS)
    shape = (x_rows.shape[0], HALF)
    return pl.pallas_call(
        partial(cut_kernel, half),
        in_specs=[SMEM, ANY],
        out_specs=[ANY] * count,
        out_shape=[jax.ShapeDtypeStruct(shape, BF16)] * count,
        scratch_shapes=[
            pltpu.VMEM((count,) + shape, BF16),
            pltpu.SemaphoreType.DMA((2, count)),
        ],
        compiler_params=params(),
        name="cut",
    )(dest, x_rows)


def pack_x_kernel(half, slot_ref, from_ref, x_ref, *rest):
    arrived, (out_ref, held, sems) = rest[: len(SHIFTS)], rest[-3:]
    count = len(arrived)
    at = pl.multiple_of(from_ref[count] * WIDTH + half * HALF, HALF)
    ins, copies = [], []
    for i in range(count + 1):
        for r in range(2):
            n = 2 * i + r
            slot = slot_ref[from_ref[i] * 2 + r]
            rows = pl.ds(r * PIECE, PIECE)
            piece = arrived[i].at[rows, :] if i < count else x_ref.at[rows, pl.ds(at, HALF)]
            ins.append(pltpu.make_async_copy(piece, held.at[n], sems.at[0, n]))
            copies.append(pltpu.make_async_copy(held.at[n], out_ref.at[slot], sems.at[1, n]))
    for copy in ins:
        copy.start()
    for n, copy in enumerate(ins):
        copy.wait()
        copies[n].start()
    for copy in copies:
        copy.wait()


def pack_x(half, slot, origin, x_rows, arrived, after):
    return pl.pallas_call(
        partial(pack_x_kernel, half),
        in_specs=[SMEM, SMEM] + [ANY] * (1 + len(arrived) + len(after)),
        out_specs=ANY,
        out_shape=jax.ShapeDtypeStruct((2 * OWNERS, PIECE, HALF), BF16),
        scratch_shapes=[
            pltpu.VMEM((2 * PEERS, PIECE, HALF), BF16),
            pltpu.SemaphoreType.DMA((2, 2 * PEERS)),
        ],
        compiler_params=params(),
        name="pack_x",
    )(slot, origin, x_rows, *arrived, *after)


def split_two(value):
    high = value.astype(BF16)
    return high, (value - high.astype(F32)).astype(BF16)


def softplus(value):
    small = jnp.exp(-jnp.abs(value))
    series = small * (1.0 - small * (0.5 - small * (1.0 / 3.0 - small * 0.25)))
    return jnp.maximum(value, 0.0) + jnp.where(small < 1e-2, series, jnp.log(1.0 + small))


def decay_kernel(src_ref, small_ref, seg_ref, bias_ref, alog_ref, *rest):
    b_ref, c_ref, bt_ref, ct_ref, rows_ref, cols_ref, scale_ref, ends_ref, total_ref, dt_ref, sems = rest
    pieces = seg_ref.shape[0]
    copies = []
    for k in range(pieces):
        for at, to in enumerate((dt_ref, b_ref, c_ref)):
            start, size = ((2 * PIECE, HEADS), (0, PIECE), (PIECE, PIECE))[at]
            rows = small_ref.at[src_ref[0, k], pl.ds(start, size), :]
            copies.append(pltpu.make_async_copy(rows, to.at[k], sems.at[at, k]))
    for copy in copies:
        copy.start()
    for copy in copies:
        copy.wait()
    step_all = softplus(dt_ref[...].astype(F32) + bias_ref[...][None])
    rate_all = -step_all * (jnp.exp(alog_ref[...]) * LOG2E)[None]
    up_to = (
        lax.broadcasted_iota(jnp.int32, (PIECE, PIECE), 0)
        <= lax.broadcasted_iota(jnp.int32, (PIECE, PIECE), 1)
    ).astype(F32)
    log_all = jnp.dot(
        rate_all.reshape(pieces * HEADS, PIECE),
        up_to,
        precision=lax.Precision.HIGHEST,
        preferred_element_type=F32,
    ).reshape(pieces, HEADS, PIECE)
    ends = [log_all[k, :, PIECE - 1 :] for k in range(pieces)]
    starts = [seg_ref[k, :, PIECE - 1 :] for k in range(pieces)]
    none = jnp.zeros((1, 1), F32)
    log_before, starts_before = [jnp.zeros((HEADS, 1), F32)], [none]
    log_after, starts_after = [jnp.zeros((HEADS, 1), F32)], [none]
    for k in range(pieces):
        log_before.append(log_before[-1] + ends[k])
        starts_before.append(starts_before[-1] + starts[k])
        log_after.append(log_after[-1] + ends[pieces - 1 - k])
        starts_after.append(starts_after[-1] + starts[pieces - 1 - k])
    rest_rows = jnp.zeros((PIECE - 3 * HEADS - 1, PIECE), F32)
    head = lax.broadcasted_iota(jnp.int32, (HEADS, WIDTH), 0)
    lane = lax.broadcasted_iota(jnp.int32, (HEADS, WIDTH), 1)
    spread_one = (lane // HEAD_DIM == head).astype(BF16)
    for k in range(pieces):
        log, step, seg = log_all[k], step_all[k], seg_ref[k]
        shifted = log - jnp.log(step) * LOG2E
        rows = jnp.concatenate([log, shifted, step, seg, rest_rows], axis=0)
        rows_ref[k] = rows[0:ROW_COUNT]
        cols_ref[k] = rows.T
        bt_ref[k] = b_ref[k].astype(F32).T.astype(BF16)
        ct_ref[k] = c_ref[k].astype(F32).T.astype(BF16)
        none_yet = (seg == 0.0).astype(F32)
        none_left = (seg == starts[k]).astype(F32)
        left = pieces - 1 - k
        entry = jnp.exp2(log) * none_yet
        step_exit = step * (jnp.exp2(ends[k] - log) * none_left)
        no_before = none_yet * (starts_before[k] == 0.0).astype(F32)
        before = jnp.exp2(log_before[k] + log) * no_before
        no_after = none_left * (starts_after[left] == 0.0).astype(F32)
        after = step * (jnp.exp2(log_after[left] + (ends[k] - log)) * no_after)
        parts = []
        for value in (entry, step_exit, before, after):
            high = value.astype(BF16).astype(F32)
            parts += [high, value - high]
        scale_ref[k] = jnp.concatenate(parts, axis=0).T.astype(BF16)
        decay = jnp.exp2(ends[k]) * (starts[k] == 0.0).astype(F32)
        high, low = split_two(jnp.broadcast_to(decay, (HEADS, PIECE)))
        ends_ref[k] = (over_first(high, spread_one) + over_first(low, spread_one))[0:8]
    total_ref[...] = jnp.broadcast_to(
        jnp.exp2(log_before[-1]) * (starts_before[-1] == 0.0).astype(F32), total_ref.shape
    )


ROW_COUNT = 56
SEG = 3 * HEADS
ENTRY, STEP_EXIT, BEFORE, AFTER = range(4)
GROUP = 256
RUN = 4


def decays(src, small, seg, bias, alog):
    pieces = seg.shape[0]
    square = (pieces, PIECE, PIECE)
    return pl.pallas_call(
        decay_kernel,
        in_specs=[SMEM, ANY, WHOLE, WHOLE, WHOLE],
        out_specs=[WHOLE] * 9,
        out_shape=[
            jax.ShapeDtypeStruct(square, BF16),
            jax.ShapeDtypeStruct(square, BF16),
            jax.ShapeDtypeStruct(square, BF16),
            jax.ShapeDtypeStruct(square, BF16),
            jax.ShapeDtypeStruct((pieces, ROW_COUNT, PIECE), F32),
            jax.ShapeDtypeStruct(square, F32),
            jax.ShapeDtypeStruct(square, BF16),
            jax.ShapeDtypeStruct((pieces, 8, WIDTH), F32),
            jax.ShapeDtypeStruct((HEADS, PIECE), F32),
        ],
        scratch_shapes=[
            pltpu.VMEM((pieces, HEADS, PIECE), BF16),
            pltpu.SemaphoreType.DMA((3, pieces)),
        ],
        compiler_params=params(),
        name="decays",
    )(src, small, seg, bias, alog)


def spread(kinds):
    shape = (kinds, kinds * 2 * HEADS, WIDTH)
    rows = lax.broadcasted_iota(jnp.int32, shape, 1)
    kind = lax.broadcasted_iota(jnp.int32, shape, 0)
    head = lax.broadcasted_iota(jnp.int32, shape, 2) // HEAD_DIM
    return ((rows // (2 * HEADS) == kind) & (rows % HEADS == head)).astype(BF16)


def over_first(left, right):
    return lax.dot_general(left, right, (((0,), (0,)), ((), ())), preferred_element_type=F32)


def dot(left, right):
    return jnp.dot(left, right, preferred_element_type=F32)


def two_heads(weights, values):
    lane = lax.broadcasted_iota(jnp.int32, values.shape, 1)
    zero = jnp.zeros_like(values)
    stacked = jnp.concatenate(
        [jnp.where(lane < HEAD_DIM, values, zero), jnp.where(lane < HEAD_DIM, zero, values)], axis=0
    )
    return dot(jnp.concatenate(weights, axis=1), stacked)


def local_piece(forward, first, r, left, turned, values_of, rows_ref, cols_ref, scale_ref, ends_ref, spread_ref, skip_ref, out_ref, state):
    scales, by_token = scale_ref[r], cols_ref[r]
    row = lax.broadcasted_iota(jnp.int32, (PIECE, PIECE), 0)
    col = lax.broadcasted_iota(jnp.int32, (PIECE, PIECE), 1)
    same = by_token[:, SEG : SEG + 1] == rows_ref[r, SEG : SEG + 1, :]
    reach = (col <= row) if forward else (col >= row)
    scores = jnp.where(reach & same, dot(left, turned), 0.0)
    into, out_of = (ENTRY, STEP_EXIT) if forward else (STEP_EXIT, ENTRY)
    for group in range(out_ref.shape[2] // GROUP):
        cols = slice(group * GROUP, (group + 1) * GROUP)
        values = values_of(group)
        near = []
        for pair in range(2):
            weights = []
            for head in (first + 4 * group + 2 * pair, first + 4 * group + 2 * pair + 1):
                if forward:
                    gap = by_token[:, head : head + 1] - rows_ref[r, HEADS + head : HEADS + head + 1, :]
                else:
                    gap = rows_ref[r, head : head + 1, :] - by_token[:, head : head + 1]
                weights.append((scores * jnp.exp2(jnp.minimum(gap, 8.0))).astype(BF16))
            part = two_heads(weights, values[:, pair * 128 : (pair + 1) * 128])
            if not forward:
                at = 2 * HEADS + head
                lane = lax.broadcasted_iota(jnp.int32, part.shape, 1)
                part *= jnp.where(lane < HEAD_DIM, by_token[:, at - 1 : at], by_token[:, at : at + 1])
            near.append(part)
        wide = values.astype(F32)
        held = state[:, cols]
        out = jnp.concatenate(near, axis=1) + skip_ref[:, cols] * wide
        out += dot(scales, spread_ref[into, :, cols]) * dot(left, held.astype(BF16))
        out_ref[r, :, cols] = out
        scaled = (wide * dot(scales, spread_ref[out_of, :, cols])).astype(BF16)
        state[:, cols] = ends_ref[r, 0:1, cols] * held + dot(turned, scaled)


def forward_kernel(half, c_ref, bt_ref, *rest):
    x_refs, (after_ref, out_ref, state) = rest[:RUN], rest[-3:]

    @pl.when(pl.program_id(0) == 0)
    def _():
        state[...] = jnp.zeros_like(state)

    for r in range(RUN):

        def values_of(group):
            return x_refs[r][0, :, group * GROUP : (group + 1) * GROUP]

        local_piece(
            True, half * HEADS // 2, r, c_ref[r], bt_ref[r], values_of, *rest[RUN:-3], out_ref, state
        )


def backward_kernel(b_ref, ct_ref, cot_ref, *rest):
    after_ref, out_ref, state = rest[-3:]

    @pl.when(pl.program_id(0) == 0)
    def _():
        state[...] = jnp.zeros_like(state)

    for r in reversed(range(RUN)):

        def values_of(group):
            return cot_ref[r * PIECE : (r + 1) * PIECE, group * GROUP : (group + 1) * GROUP]

        local_piece(False, 0, r, b_ref[r], ct_ref[r], values_of, *rest[:-3], out_ref, state)


def local_call(kernel, place, width, half, firsts, specs, values, src, local, after, name):
    rows, cols, scales, ends, spread_four, skip = local
    pieces = rows.shape[0]
    at = lambda k, src: (place(k), 0, 0)
    square = pl.BlockSpec((RUN, PIECE, PIECE), at)
    return pl.pallas_call(
        skip_src(kernel),
        grid_spec=pltpu.PrefetchScalarGridSpec(
            num_scalar_prefetch=1,
            grid=(pieces // RUN,),
            in_specs=[
                square,
                square,
                *specs,
                pl.BlockSpec((RUN, ROW_COUNT, PIECE), at),
                square,
                square,
                pl.BlockSpec((RUN, 8, width), lambda k, src: (place(k), 0, half)),
                pl.BlockSpec(spread_four.shape[:2] + (width,), lambda k, src: (0, 0, half)),
                pl.BlockSpec((1, width), lambda k, src: (0, half)),
                ANY,
            ],
            out_specs=pl.BlockSpec((RUN, PIECE, width), at),
            scratch_shapes=[pltpu.VMEM((STATE, width), F32)],
        ),
        out_shape=jax.ShapeDtypeStruct((pieces, PIECE, width), F32),
        compiler_params=params(),
        name=name,
    )(src, *firsts, *values, rows, cols, scales, ends, spread_four, skip, after)


def skip_src(kernel):
    return lambda src_ref, *refs: kernel(*refs)


def forward_local(half, src, c, bt, x_slots, local, after):
    specs = [
        pl.BlockSpec((1, PIECE, HALF), lambda k, src, r=r: (src[0, RUN * k + r], 0, 0))
        for r in range(RUN)
    ]
    kernel = partial(forward_kernel, half)
    values = [x_slots[half]] * RUN
    return local_call(
        kernel, lambda k: k, HALF, half, [c, bt], specs, values, src, local, after, "forward_local"
    )


def backward_local(src, b, ct, cotangent, local, after):
    last = b.shape[0] // RUN - 1
    specs = [pl.BlockSpec((RUN * PIECE, WIDTH), lambda k, src: (last - k, 0))]
    place = lambda k: last - k
    return local_call(
        backward_kernel, place, WIDTH, 0, [b, ct], specs, [cotangent], src, local, after, "backward_local"
    )


def leaving_state(kind, keys_ref, v_all, scale_ref, spread_ref, store):
    pieces = scale_ref.shape[0]
    for group in range(WIDTH // GROUP):
        cols = slice(group * GROUP, (group + 1) * GROUP)
        state = None
        for k in range(0, pieces, 4):
            scales = scale_ref[k : k + 4].reshape(4 * PIECE, PIECE)
            scale = dot(scales, spread_ref[kind, :, cols])
            values = v_all[k : k + 4, :, cols].reshape(4 * PIECE, GROUP)
            scaled = (values.astype(F32) * scale).astype(BF16)
            for r in range(4):
                update = dot(keys_ref[k + r], scaled[r * PIECE : (r + 1) * PIECE])
                state = update if state is None else state + update
        store(cols, state.astype(BF16))


def leaving_gradient_kernel(cot_ref, keys_ref, scale_ref, spread_ref, out_ref):
    def store(cols, value):
        out_ref[:, cols] = value

    leaving_state(BEFORE, keys_ref, cot_ref, scale_ref, spread_ref, store)


def leaving_gradient(keys, cotangent, scales, spread_four):
    pieces = scales.shape[0]
    return pl.pallas_call(
        leaving_gradient_kernel,
        out_shape=jax.ShapeDtypeStruct((STATE, WIDTH), BF16),
        compiler_params=params(),
        name="leaving_gradient",
    )(cotangent.reshape(pieces, PIECE, WIDTH), keys, scales, spread_four)


def leaving_kernel(src_ref, xa_ref, xb_ref, keys_ref, scale_ref, spread_ref, g_ref, total_ref, out_ref, v_all, sems):
    ins = []
    for k in range(scale_ref.shape[0]):
        for half, ref in enumerate((xa_ref, xb_ref)):
            to = v_all.at[k, :, pl.ds(half * HALF, HALF)]
            ins.append(pltpu.make_async_copy(ref.at[src_ref[0, k]], to, sems.at[half, k]))
    for copy in ins:
        copy.start()
    high, low = split_two(total_ref[...])
    lane = lax.broadcasted_iota(jnp.int32, high.shape, 1)
    decay = jnp.where(lane == 0, high, jnp.where(lane == 1, low, jnp.zeros_like(low)))
    for part in range(OWNERS):
        out_ref[part, :, WIDTH:] = decay
        if part >= 8:
            out_ref[part, :, 0:WIDTH] = g_ref[part % 8 * 16 : part % 8 * 16 + 16, :]
    for copy in ins:
        copy.wait()

    def store(cols, value):
        for part in range(8):
            out_ref[part, :, cols] = value[part * 16 : part * 16 + 16]

    leaving_state(AFTER, keys_ref, v_all, scale_ref, spread_ref, store)


def leaving(src, x_slots, keys, scales, spread_four, g_state, total):
    pieces = scales.shape[0]
    return pl.pallas_call(
        leaving_kernel,
        in_specs=[SMEM, ANY, ANY] + [WHOLE] * 5,
        out_specs=WHOLE,
        out_shape=jax.ShapeDtypeStruct((OWNERS, 16, WIDTH + EXTRA), BF16),
        scratch_shapes=[
            pltpu.VMEM((pieces, PIECE, WIDTH), BF16),
            pltpu.SemaphoreType.DMA((2, pieces)),
        ],
        compiler_params=params(),
        name="leaving",
    )(src, *x_slots, keys, scales, spread_four, g_state, total)


def scan_kernel(back_ref, part_ref, after_ref, out_ref):
    back = back_ref[0]
    head = lax.broadcasted_iota(jnp.int32, (HEADS, WIDTH), 0)
    lane = lax.broadcasted_iota(jnp.int32, (HEADS, WIDTH), 1)
    spread_one = (lane // HEAD_DIM == head).astype(BF16)
    held = jnp.zeros((HEADS, WIDTH), F32)
    for k in range(OWNERS):
        at = jnp.where(back == 1, OWNERS - 1 - k, k)
        out_ref[at] = held.astype(BF16)
        decay = over_first(part_ref[at, :, WIDTH:], spread_one)
        held = (decay[0:1] + decay[1:2]) * held + part_ref[at, :, 0:WIDTH].astype(F32)


def scan_owners(back, parts, after):
    return pl.pallas_call(
        scan_kernel,
        in_specs=[SMEM, WHOLE, ANY],
        out_specs=WHOLE,
        out_shape=jax.ShapeDtypeStruct((OWNERS, 16, WIDTH), BF16),
        compiler_params=params(),
        name="scan_owners",
    )(back, parts, after)


def finish_kernel(b_ref, c_ref, ya_ref, yb_ref, g_ref, enter_ref, scale_ref, spread_ref, y_out, g_out):
    rows = 2 * PIECE
    b, c, scales = b_ref[...].reshape(rows, STATE), c_ref[...].reshape(rows, STATE), scale_ref[...].reshape(rows, PIECE)
    for group in range(WIDTH // GROUP):
        cols = slice(group * GROUP, (group + 1) * GROUP)
        y_off = dot(scales, spread_ref[BEFORE, :, cols]) * dot(c, enter_ref[0:STATE, cols])
        start = group % 2 * GROUP
        y = (ya_ref if group < 2 else yb_ref)[:, :, start : start + GROUP].reshape(rows, GROUP)
        y_out[:, cols] = (y + y_off).astype(BF16)
        g_off = dot(scales, spread_ref[AFTER, :, cols]) * dot(b, enter_ref[STATE:, cols])
        g_out[:, cols] = (g_ref[:, :, cols].reshape(rows, GROUP) + g_off).astype(BF16)


def finish(b, c, y_a, y_b, g_local, enter, scales, spread_four):
    pieces = scales.shape[0]
    out = jax.ShapeDtypeStruct((pieces * PIECE, WIDTH), BF16)
    square = pl.BlockSpec((2, PIECE, PIECE), lambda k: (k, 0, 0))
    half = pl.BlockSpec((2, PIECE, HALF), lambda k: (k, 0, 0))
    wide = pl.BlockSpec((2, PIECE, WIDTH), lambda k: (k, 0, 0))
    return pl.pallas_call(
        finish_kernel,
        grid=(pieces // 2,),
        in_specs=[
            square,
            square,
            half,
            half,
            wide,
            pl.BlockSpec((2 * STATE, WIDTH), lambda k: (0, 0)),
            square,
            pl.BlockSpec(spread_four.shape, lambda k: (0, 0, 0)),
        ],
        out_specs=[pl.BlockSpec((2 * PIECE, WIDTH), lambda k: (k, 0))] * 2,
        out_shape=[out, out],
        compiler_params=params(),
        name="finish",
    )(b, c, y_a, y_b, g_local, enter, scales, spread_four)


def ranks(dest):
    owner = dest // OWNERS
    here = lax.broadcasted_iota(jnp.int32, (OWNERS, OWNERS), 0)
    other = lax.broadcasted_iota(jnp.int32, (OWNERS, OWNERS), 1)
    same = (owner[..., None, :] == owner[..., :, None]) & (other < here)
    return jnp.sum(same.astype(jnp.int32), axis=-1)


def to_owners(value):
    return lax.all_to_all(value, "ctx", split_axis=0, concat_axis=0, tiled=True)


def body(
    x_rows, b_rows, c_rows, dt_rows, destination, doc_start, a_log, dt_bias, d_skip, cotangent
):
    head = lax.axis_index("head")
    me = lax.axis_index("ctx")
    dest_heads = jnp.stack([partner(head, s) for s in SHIFTS]).astype(jnp.int32)
    origin = jnp.stack([source(head, s) for s in SHIFTS] + [head]).astype(jnp.int32)
    send_slot = destination // OWNERS * 2 + ranks(destination)

    small = gather_small(b_rows, c_rows, dt_rows)
    small = lax.all_to_all(small, "head", split_axis=0, concat_axis=0, tiled=True)
    small = small.reshape(OWNERS, SMALL_ROWS, STATE)
    small = to_owners(pack_small(send_slot, destination % OWNERS, small))
    src = find_source(small)
    pieces = destination.shape[0]
    seg = jnp.cumsum(doc_start.reshape(pieces, PIECE), axis=1).astype(F32)[:, None, :]
    b, c, bt, ct, rows, cols, scales, ends, total = decays(
        src, small, seg, dt_bias.reshape(HEADS, 1), a_log.reshape(HEADS, 1)
    )
    skip = jnp.repeat(d_skip, HEAD_DIM).reshape(1, WIDTH)
    spread_four = spread(4)
    local = (rows, cols, scales, ends, spread_four, skip)

    x_slots = []
    after = []
    for half in range(2):
        arrived = []
        for shift, piece in zip(SHIFTS, cut(half, dest_heads, x_rows)):
            pairs = [(h, partner(h, shift)) for h in range(PEERS)]
            arrived.append(lax.ppermute(piece, "head", pairs))
        x_slots.append(to_owners(pack_x(half, send_slot, origin, x_rows, arrived, after)))
        if half == 0:
            g_state = leaving_gradient(ct, cotangent, scales, spread_four)
            g_local = backward_local(src, b, ct, cotangent, local, g_state)
            after = [g_local]

    parts = leaving(src, x_slots, bt, scales, spread_four, g_state, total)
    y_a = forward_local(0, src, c, bt, x_slots, local, parts)
    back = (me >= OWNERS // 2).astype(jnp.int32).reshape(1)
    enter = scan_owners(back, to_owners(parts), y_a)
    y_b = forward_local(1, src, c, bt, x_slots, local, enter)
    enter = to_owners(enter).reshape(2 * STATE, WIDTH)
    return tuple(finish(b, c, y_a, y_b, g_local, enter, scales, spread_four))


def solution(mesh):
    in_specs = (
        P(("ctx", "head"), None),
        P(("ctx", "head"), None),
        P(("ctx", "head"), None),
        P(("ctx", "head"), None),
        P("ctx"),
        P("ctx"),
        P("head"),
        P("head"),
        P("head"),
        P("ctx", "head"),
    )
    out_specs = (P("ctx", "head"), P("ctx", "head"))
    return jax.shard_map(body, mesh=mesh, in_specs=in_specs, out_specs=out_specs, check_vma=False)
```

```python
from functools import partial

import jax
import jax.numpy as jnp
from jax import lax
from jax.experimental import pallas as pl
from jax.experimental.pallas import tpu as pltpu
from jax.sharding import PartitionSpec as P

OWNERS = 16
PEERS = 8
PIECE = 128
STATE = 128
HEADS = 16
HEAD_DIM = 64
WIDTH = HEADS * HEAD_DIM
HALF = WIDTH // 2
SMALL_ROWS = 2 * PIECE + HEADS
TAG_ROWS = 16
SENT_ROWS = SMALL_ROWS + TAG_ROWS
EXTRA = 128
LOG2E = 1.4426950408889634
F32 = jnp.float32
BF16 = jnp.bfloat16
ANY = pl.BlockSpec(memory_space=pl.ANY)
WHOLE = pl.BlockSpec(memory_space=pltpu.VMEM)
SMEM = pl.BlockSpec(memory_space=pltpu.SMEM)
EARLY = 2
SHIFTS = [(1, 0), (3, 0), (1, 1), (3, 1), (2, 0), (2, 1), (0, 1)]


def params(mib=56):
    return pltpu.CompilerParams(vmem_limit_bytes=mib * 1024 * 1024)


def partner(head, shift):
    return (head // 2 + shift[0]) % 4 * 2 + (head % 2 + shift[1]) % 2


def source(head, shift):
    return (head // 2 + 4 - shift[0]) % 4 * 2 + (head % 2 + shift[1]) % 2


def run_copies(copies):
    for copy in copies:
        copy.start()
    for copy in copies:
        copy.wait()


def gather_small_kernel(b_ref, c_ref, dt_ref, out_ref, turned, sems):
    copies = []
    for r in range(2):
        rows = pl.ds(r * PIECE, PIECE)
        for g in range(PEERS):
            cols = pl.ds(g * STATE, STATE)
            for kind, ref in enumerate((b_ref, c_ref)):
                copies.append(
                    pltpu.make_async_copy(
                        ref.at[rows, cols],
                        out_ref.at[g, r, pl.ds(kind * PIECE, PIECE), :],
                        sems.at[len(copies)],
                    )
                )
    for copy in copies:
        copy.start()
    last = []
    for r in range(2):
        dt_t = dt_ref[r * PIECE : (r + 1) * PIECE, :].astype(F32).T.astype(BF16)
        for g in range(PEERS):
            turned[g, r] = dt_t[g * HEADS : (g + 1) * HEADS, :]
    last = pltpu.make_async_copy(
        turned, out_ref.at[:, :, pl.ds(2 * PIECE, HEADS), :], sems.at[len(copies)]
    )
    last.start()
    for copy in copies + [last]:
        copy.wait()


def gather_small(b_rows, c_rows, dt_rows):
    return pl.pallas_call(
        gather_small_kernel,
        in_specs=[WHOLE, WHOLE, WHOLE],
        out_specs=ANY,
        out_shape=jax.ShapeDtypeStruct((PEERS, 2, SMALL_ROWS, STATE), BF16),
        scratch_shapes=[
            pltpu.VMEM((PEERS, 2, HEADS, PIECE), BF16),
            pltpu.SemaphoreType.DMA((4 * PEERS + 1,)),
        ],
        compiler_params=params(),
        name="gather_small",
    )(b_rows, c_rows, dt_rows)


def pack_small_kernel(slot_ref, place_ref, in_ref, *rest):
    out_ref, tags, sems = rest[-3:]
    copies = [
        pltpu.make_async_copy(
            in_ref.at[j], out_ref.at[slot_ref[j], pl.ds(0, SMALL_ROWS), :], sems.at[j]
        )
        for j in range(OWNERS)
    ]
    for copy in copies:
        copy.start()
    tags[...] = jnp.full(tags.shape, -1.0, BF16)
    for j in range(OWNERS):
        place = place_ref[j].astype(F32)
        tags[slot_ref[j]] = jnp.full(tags.shape[1:], place, F32).astype(BF16)
    last = pltpu.make_async_copy(
        tags, out_ref.at[:, pl.ds(SMALL_ROWS, TAG_ROWS), :], sems.at[OWNERS]
    )
    last.start()
    for copy in copies + [last]:
        copy.wait()


def pack_small(slot, place, pieces, after):
    return pl.pallas_call(
        pack_small_kernel,
        in_specs=[SMEM, SMEM, WHOLE] + [ANY] * len(after),
        out_specs=ANY,
        out_shape=jax.ShapeDtypeStruct((2 * OWNERS, SENT_ROWS, STATE), BF16),
        scratch_shapes=[
            pltpu.VMEM((2 * OWNERS, TAG_ROWS, STATE), BF16),
            pltpu.SemaphoreType.DMA((OWNERS + 1,)),
        ],
        compiler_params=params(),
        name="pack_small",
    )(slot, place, pieces, *after)


def find_source_kernel(small_ref, out_ref, tags, sem):
    copy = pltpu.make_async_copy(
        small_ref.at[:, pl.ds(SMALL_ROWS, TAG_ROWS), :], tags, sem.at[0]
    )
    copy.start()
    copy.wait()
    slot = lax.broadcasted_iota(jnp.int32, tags.shape, 0).astype(F32)
    place = lax.broadcasted_iota(jnp.int32, tags.shape, 2).astype(F32)
    found = jnp.where(tags[...].astype(F32) == place, slot, 0.0)
    out_ref[...] = jnp.sum(found, axis=0)[0:1].astype(jnp.int32)


def find_source(small):
    return pl.pallas_call(
        find_source_kernel,
        in_specs=[ANY],
        out_specs=pl.BlockSpec(memory_space=pltpu.VMEM),
        out_shape=jax.ShapeDtypeStruct((1, STATE), jnp.int32),
        scratch_shapes=[
            pltpu.VMEM((2 * OWNERS, TAG_ROWS, STATE), BF16),
            pltpu.SemaphoreType.DMA((1,)),
        ],
        compiler_params=params(),
        name="find_source",
    )(small)


def cut_kernel(half, dest_ref, x_ref, *rest):
    count = len(SHIFTS)
    outs, (held, sems) = rest[:count], rest[count:]
    ins, copies = [], []
    for i in range(count):
        at = pl.multiple_of(dest_ref[i] * WIDTH + half * HALF, HALF)
        ins.append(pltpu.make_async_copy(x_ref.at[:, pl.ds(at, HALF)], held.at[i], sems.at[0, i]))
        copies.append(pltpu.make_async_copy(held.at[i], outs[i], sems.at[1, i]))
    for copy in ins:
        copy.start()
    for i in range(count):
        ins[i].wait()
        copies[i].start()
    for copy in copies:
        copy.wait()


def cut(half, dest, x_rows):
    count = len(SHIFTS)
    shape = (x_rows.shape[0], HALF)
    return pl.pallas_call(
        partial(cut_kernel, half),
        in_specs=[SMEM, ANY],
        out_specs=[ANY] * count,
        out_shape=[jax.ShapeDtypeStruct(shape, BF16)] * count,
        scratch_shapes=[
            pltpu.VMEM((count,) + shape, BF16),
            pltpu.SemaphoreType.DMA((2, count)),
        ],
        compiler_params=params(),
        name="cut",
    )(dest, x_rows)


def pack_x_kernel(half, slot_ref, from_ref, x_ref, *rest):
    arrived, (out_ref, held, sems) = rest[: len(SHIFTS)], rest[-3:]
    count = len(arrived)
    at = pl.multiple_of(from_ref[count] * WIDTH + half * HALF, HALF)
    ins, copies = [], []
    for i in range(count + 1):
        for r in range(2):
            n = 2 * i + r
            slot = slot_ref[from_ref[i] * 2 + r]
            rows = pl.ds(r * PIECE, PIECE)
            piece = arrived[i].at[rows, :] if i < count else x_ref.at[rows, pl.ds(at, HALF)]
            ins.append(pltpu.make_async_copy(piece, held.at[n], sems.at[0, n]))
            copies.append(pltpu.make_async_copy(held.at[n], out_ref.at[slot], sems.at[1, n]))
    for copy in ins:
        copy.start()
    for n, copy in enumerate(ins):
        copy.wait()
        copies[n].start()
    for copy in copies:
        copy.wait()


def pack_x(half, slot, origin, x_rows, arrived, after):
    return pl.pallas_call(
        partial(pack_x_kernel, half),
        in_specs=[SMEM, SMEM] + [ANY] * (1 + len(arrived) + len(after)),
        out_specs=ANY,
        out_shape=jax.ShapeDtypeStruct((2 * OWNERS, PIECE, HALF), BF16),
        scratch_shapes=[
            pltpu.VMEM((2 * PEERS, PIECE, HALF), BF16),
            pltpu.SemaphoreType.DMA((2, 2 * PEERS)),
        ],
        compiler_params=params(),
        name="pack_x",
    )(slot, origin, x_rows, *arrived, *after)


def hold_kernel(value_ref, *rest):
    del value_ref, rest


def hold(value, after):
    return pl.pallas_call(
        hold_kernel,
        in_specs=[ANY] * (1 + len(after)),
        out_specs=ANY,
        out_shape=jax.ShapeDtypeStruct(value.shape, value.dtype),
        input_output_aliases={0: 0},
        compiler_params=params(),
        name="hold",
    )(value, *after)


def split_two(value):
    high = value.astype(BF16)
    return high, (value - high.astype(F32)).astype(BF16)


def softplus(value):
    small = jnp.exp(-jnp.abs(value))
    series = small * (1.0 - small * (0.5 - small * (1.0 / 3.0 - small * 0.25)))
    return jnp.maximum(value, 0.0) + jnp.where(small < 1e-2, series, jnp.log(1.0 + small))


def decay_kernel(src_ref, small_ref, seg_ref, bias_ref, alog_ref, *rest):
    b_ref, c_ref, bt_ref, ct_ref, rows_ref, cols_ref, scale_ref, ends_ref, total_ref, dt_ref, sems = rest
    pieces = seg_ref.shape[0]
    copies = []
    for k in range(pieces):
        for at, to in enumerate((dt_ref, b_ref, c_ref)):
            start, size = ((2 * PIECE, HEADS), (0, PIECE), (PIECE, PIECE))[at]
            rows = small_ref.at[src_ref[0, k], pl.ds(start, size), :]
            copies.append(pltpu.make_async_copy(rows, to.at[k], sems.at[at, k]))
    for copy in copies:
        copy.start()
    for copy in copies:
        copy.wait()
    step_all = softplus(dt_ref[...].astype(F32) + bias_ref[...][None])
    rate_all = -step_all * (jnp.exp(alog_ref[...]) * LOG2E)[None]
    up_to = (
        lax.broadcasted_iota(jnp.int32, (PIECE, PIECE), 0)
        <= lax.broadcasted_iota(jnp.int32, (PIECE, PIECE), 1)
    ).astype(F32)
    log_all = jnp.dot(
        rate_all.reshape(pieces * HEADS, PIECE),
        up_to,
        precision=lax.Precision.HIGHEST,
        preferred_element_type=F32,
    ).reshape(pieces, HEADS, PIECE)
    ends = [log_all[k, :, PIECE - 1 :] for k in range(pieces)]
    starts = [seg_ref[k, :, PIECE - 1 :] for k in range(pieces)]
    none = jnp.zeros((1, 1), F32)
    log_before, starts_before = [jnp.zeros((HEADS, 1), F32)], [none]
    log_after, starts_after = [jnp.zeros((HEADS, 1), F32)], [none]
    for k in range(pieces):
        log_before.append(log_before[-1] + ends[k])
        starts_before.append(starts_before[-1] + starts[k])
        log_after.append(log_after[-1] + ends[pieces - 1 - k])
        starts_after.append(starts_after[-1] + starts[pieces - 1 - k])
    rest_rows = jnp.zeros((PIECE - 3 * HEADS - 1, PIECE), F32)
    head = lax.broadcasted_iota(jnp.int32, (HEADS, WIDTH), 0)
    lane = lax.broadcasted_iota(jnp.int32, (HEADS, WIDTH), 1)
    spread_one = (lane // HEAD_DIM == head).astype(BF16)
    for k in range(pieces):
        log, step, seg = log_all[k], step_all[k], seg_ref[k]
        shifted = log - jnp.log(step) * LOG2E
        rows = jnp.concatenate([log, shifted, step, seg, rest_rows], axis=0)
        rows_ref[k] = rows[0:ROW_COUNT]
        cols_ref[k] = rows.T
        bt_ref[k] = b_ref[k].astype(F32).T.astype(BF16)
        ct_ref[k] = c_ref[k].astype(F32).T.astype(BF16)
        none_yet = (seg == 0.0).astype(F32)
        none_left = (seg == starts[k]).astype(F32)
        left = pieces - 1 - k
        entry = jnp.exp2(log) * none_yet
        step_exit = step * (jnp.exp2(ends[k] - log) * none_left)
        no_before = none_yet * (starts_before[k] == 0.0).astype(F32)
        before = jnp.exp2(log_before[k] + log) * no_before
        no_after = none_left * (starts_after[left] == 0.0).astype(F32)
        after = step * (jnp.exp2(log_after[left] + (ends[k] - log)) * no_after)
        parts = []
        for value in (entry, step_exit, before, after):
            high = value.astype(BF16).astype(F32)
            parts += [high, value - high]
        scale_ref[k] = jnp.concatenate(parts, axis=0).T.astype(BF16)
        decay = jnp.exp2(ends[k]) * (starts[k] == 0.0).astype(F32)
        high, low = split_two(jnp.broadcast_to(decay, (HEADS, PIECE)))
        ends_ref[k] = (over_first(high, spread_one) + over_first(low, spread_one))[0:8]
    total = jnp.exp2(log_before[-1]) * (starts_before[-1] == 0.0).astype(F32)
    total = jnp.broadcast_to(total, (HEADS, PIECE))
    high = total.astype(BF16).astype(F32)
    blank = jnp.zeros((PIECE - 2 * HEADS, PIECE), F32)
    total_ref[...] = jnp.concatenate([high, total - high, blank], axis=0).T[0:16].astype(BF16)


ROW_COUNT = 56
SEG = 3 * HEADS
ENTRY, STEP_EXIT, BEFORE, AFTER = range(4)
GROUP = 256
RUN = 4


def decays(src, small, seg, bias, alog):
    pieces = seg.shape[0]
    square = (pieces, PIECE, PIECE)
    return pl.pallas_call(
        decay_kernel,
        in_specs=[SMEM, ANY, WHOLE, WHOLE, WHOLE],
        out_specs=[WHOLE] * 9,
        out_shape=[
            jax.ShapeDtypeStruct(square, BF16),
            jax.ShapeDtypeStruct(square, BF16),
            jax.ShapeDtypeStruct(square, BF16),
            jax.ShapeDtypeStruct(square, BF16),
            jax.ShapeDtypeStruct((pieces, ROW_COUNT, PIECE), F32),
            jax.ShapeDtypeStruct(square, F32),
            jax.ShapeDtypeStruct(square, BF16),
            jax.ShapeDtypeStruct((pieces, 8, WIDTH), F32),
            jax.ShapeDtypeStruct((16, EXTRA), BF16),
        ],
        scratch_shapes=[
            pltpu.VMEM((pieces, HEADS, PIECE), BF16),
            pltpu.SemaphoreType.DMA((3, pieces)),
        ],
        compiler_params=params(),
        name="decays",
    )(src, small, seg, bias, alog)


def spread(kinds):
    shape = (kinds, kinds * 2 * HEADS, WIDTH)
    rows = lax.broadcasted_iota(jnp.int32, shape, 1)
    kind = lax.broadcasted_iota(jnp.int32, shape, 0)
    head = lax.broadcasted_iota(jnp.int32, shape, 2) // HEAD_DIM
    return ((rows // (2 * HEADS) == kind) & (rows % HEADS == head)).astype(BF16)


def over_first(left, right):
    return lax.dot_general(left, right, (((0,), (0,)), ((), ())), preferred_element_type=F32)


def dot(left, right):
    return jnp.dot(left, right, preferred_element_type=F32)


def two_heads(weights, values):
    lane = lax.broadcasted_iota(jnp.int32, values.shape, 1)
    zero = jnp.zeros_like(values)
    stacked = jnp.concatenate(
        [jnp.where(lane < HEAD_DIM, values, zero), jnp.where(lane < HEAD_DIM, zero, values)], axis=0
    )
    return dot(jnp.concatenate(weights, axis=1), stacked)


def local_piece(forward, first, r, left, turned, values_of, rows_ref, cols_ref, scale_ref, ends_ref, spread_ref, skip_ref, out_ref, state):
    scales, by_token = scale_ref[r], cols_ref[r]
    row = lax.broadcasted_iota(jnp.int32, (PIECE, PIECE), 0)
    col = lax.broadcasted_iota(jnp.int32, (PIECE, PIECE), 1)
    same = by_token[:, SEG : SEG + 1] == rows_ref[r, SEG : SEG + 1, :]
    reach = (col <= row) if forward else (col >= row)
    scores = jnp.where(reach & same, dot(left, turned), 0.0)
    into, out_of = (ENTRY, STEP_EXIT) if forward else (STEP_EXIT, ENTRY)
    for group in range(out_ref.shape[2] // GROUP):
        cols = slice(group * GROUP, (group + 1) * GROUP)
        values = values_of(group)
        near = []
        for pair in range(2):
            weights = []
            for head in (first + 4 * group + 2 * pair, first + 4 * group + 2 * pair + 1):
                if forward:
                    gap = by_token[:, head : head + 1] - rows_ref[r, HEADS + head : HEADS + head + 1, :]
                else:
                    gap = rows_ref[r, head : head + 1, :] - by_token[:, head : head + 1]
                weights.append((scores * jnp.exp2(jnp.minimum(gap, 8.0))).astype(BF16))
            part = two_heads(weights, values[:, pair * 128 : (pair + 1) * 128])
            if not forward:
                at = 2 * HEADS + head
                lane = lax.broadcasted_iota(jnp.int32, part.shape, 1)
                part *= jnp.where(lane < HEAD_DIM, by_token[:, at - 1 : at], by_token[:, at : at + 1])
            near.append(part)
        wide = values.astype(F32)
        held = state[:, cols]
        out = jnp.concatenate(near, axis=1) + skip_ref[:, cols] * wide
        out += dot(scales, spread_ref[into, :, cols]) * dot(left, held.astype(BF16))
        out_ref[r, :, cols] = out.astype(BF16)
        scaled = (wide * dot(scales, spread_ref[out_of, :, cols])).astype(BF16)
        state[:, cols] = ends_ref[r, 0:1, cols] * held + dot(turned, scaled)


def forward_kernel(half, c_ref, bt_ref, *rest):
    x_refs, (after_ref, out_ref, state) = rest[:RUN], rest[-3:]

    @pl.when(pl.program_id(0) == 0)
    def _():
        state[...] = jnp.zeros_like(state)

    for r in range(RUN):

        def values_of(group):
            return x_refs[r][0, :, group * GROUP : (group + 1) * GROUP]

        local_piece(
            True, half * HEADS // 2, r, c_ref[r], bt_ref[r], values_of, *rest[RUN:-3], out_ref, state
        )


def backward_kernel(b_ref, ct_ref, cot_ref, *rest):
    after_ref, out_ref, state = rest[-3:]

    @pl.when(pl.program_id(0) == 0)
    def _():
        state[...] = jnp.zeros_like(state)

    for r in reversed(range(RUN)):

        def values_of(group):
            return cot_ref[r * PIECE : (r + 1) * PIECE, group * GROUP : (group + 1) * GROUP]

        local_piece(False, 0, r, b_ref[r], ct_ref[r], values_of, *rest[:-3], out_ref, state)


def local_call(kernel, place, width, half, firsts, specs, values, src, local, after, name):
    rows, cols, scales, ends, spread_four, skip = local
    pieces = rows.shape[0]
    at = lambda k, src: (place(k), 0, 0)
    square = pl.BlockSpec((RUN, PIECE, PIECE), at)
    return pl.pallas_call(
        skip_src(kernel),
        grid_spec=pltpu.PrefetchScalarGridSpec(
            num_scalar_prefetch=1,
            grid=(pieces // RUN,),
            in_specs=[
                square,
                square,
                *specs,
                pl.BlockSpec((RUN, ROW_COUNT, PIECE), at),
                square,
                square,
                pl.BlockSpec((RUN, 8, width), lambda k, src: (place(k), 0, half)),
                pl.BlockSpec(spread_four.shape[:2] + (width,), lambda k, src: (0, 0, half)),
                pl.BlockSpec((1, width), lambda k, src: (0, half)),
                ANY,
            ],
            out_specs=pl.BlockSpec((RUN, PIECE, width), at),
            scratch_shapes=[pltpu.VMEM((STATE, width), F32)],
        ),
        out_shape=jax.ShapeDtypeStruct((pieces, PIECE, width), BF16),
        compiler_params=params(),
        name=name,
    )(src, *firsts, *values, rows, cols, scales, ends, spread_four, skip, after)


def skip_src(kernel):
    return lambda src_ref, *refs: kernel(*refs)


def forward_local(half, src, c, bt, x_slots, local, after):
    specs = [
        pl.BlockSpec((1, PIECE, HALF), lambda k, src, r=r: (src[0, RUN * k + r], 0, 0))
        for r in range(RUN)
    ]
    kernel = partial(forward_kernel, half)
    values = [x_slots[half]] * RUN
    return local_call(
        kernel, lambda k: k, HALF, half, [c, bt], specs, values, src, local, after, "forward_local"
    )


def backward_local(src, b, ct, cotangent, local, after):
    last = b.shape[0] // RUN - 1
    specs = [pl.BlockSpec((RUN * PIECE, WIDTH), lambda k, src: (last - k, 0))]
    place = lambda k: last - k
    return local_call(
        backward_kernel, place, WIDTH, 0, [b, ct], specs, [cotangent], src, local, after, "backward_local"
    )


def leaving_state(kind, keys_ref, v_all, scale_ref, spread_ref, state, wait):
    pieces = scale_ref.shape[0]
    for k in range(0, pieces, RUN):
        wait(k)
        scales = scale_ref[k : k + RUN].reshape(RUN * PIECE, PIECE)
        for group in range(WIDTH // GROUP):
            cols = slice(group * GROUP, (group + 1) * GROUP)
            scale = dot(scales, spread_ref[0, :, cols])
            values = v_all[k : k + RUN, :, cols].reshape(RUN * PIECE, GROUP)
            scaled = (values.astype(F32) * scale).astype(BF16)
            total = None if k == 0 else state[:, cols]
            for r in range(RUN):
                update = dot(keys_ref[k + r], scaled[r * PIECE : (r + 1) * PIECE])
                total = update if total is None else total + update
            state[:, cols] = total


def leaving_gradient_kernel(cot_ref, keys_ref, scale_ref, spread_ref, out_ref, v_all, state, sems):
    copies = [
        pltpu.make_async_copy(cot_ref.at[pl.ds(k * PIECE, PIECE), :], v_all.at[k], sems.at[k])
        for k in range(scale_ref.shape[0])
    ]
    for copy in copies:
        copy.start()

    def wait(k):
        for copy in copies[k : k + RUN]:
            copy.wait()

    leaving_state(BEFORE, keys_ref, v_all, scale_ref, spread_ref, state, wait)
    out_ref[...] = state[...].astype(BF16)


def kind_spec(kind):
    return pl.BlockSpec((1, PIECE, WIDTH), lambda i: (kind, 0, 0))


def leaving_gradient(keys, cotangent, scales, spread_four):
    pieces = scales.shape[0]
    return pl.pallas_call(
        leaving_gradient_kernel,
        grid=(1,),
        in_specs=[ANY, WHOLE, WHOLE, kind_spec(BEFORE)],
        out_specs=WHOLE,
        out_shape=jax.ShapeDtypeStruct((STATE, WIDTH), BF16),
        scratch_shapes=[
            pltpu.VMEM((pieces, PIECE, WIDTH), BF16),
            pltpu.VMEM((STATE, WIDTH), F32),
            pltpu.SemaphoreType.DMA((pieces,)),
        ],
        compiler_params=params(),
        name="leaving_gradient",
    )(cotangent, keys, scales, spread_four)


def leaving_kernel(src_ref, xa_ref, xb_ref, keys_ref, scale_ref, spread_ref, g_ref, total_ref, out_ref, v_all, state, sems):
    ins = []
    for k in range(scale_ref.shape[0]):
        for half, ref in enumerate((xa_ref, xb_ref)):
            to = v_all.at[k, :, pl.ds(half * HALF, HALF)]
            ins.append(pltpu.make_async_copy(ref.at[src_ref[0, k]], to, sems.at[half, k]))
    for copy in ins:
        copy.start()
    for part in range(OWNERS):
        out_ref[part, :, WIDTH:] = total_ref[...]
        if part >= 8:
            out_ref[part, :, 0:WIDTH] = g_ref[part % 8 * 16 : part % 8 * 16 + 16, :]

    def wait(k):
        for copy in ins[2 * k : 2 * (k + RUN)]:
            copy.wait()

    leaving_state(AFTER, keys_ref, v_all, scale_ref, spread_ref, state, wait)
    for part in range(8):
        out_ref[part, :, 0:WIDTH] = state[part * 16 : part * 16 + 16, :].astype(BF16)


def leaving(src, x_slots, keys, scales, spread_four, g_state, total):
    pieces = scales.shape[0]
    return pl.pallas_call(
        leaving_kernel,
        grid=(1,),
        in_specs=[SMEM, ANY, ANY, WHOLE, WHOLE, kind_spec(AFTER), WHOLE, WHOLE],
        out_specs=WHOLE,
        out_shape=jax.ShapeDtypeStruct((OWNERS, 16, WIDTH + EXTRA), BF16),
        scratch_shapes=[
            pltpu.VMEM((pieces, PIECE, WIDTH), BF16),
            pltpu.VMEM((STATE, WIDTH), F32),
            pltpu.SemaphoreType.DMA((2, pieces)),
        ],
        compiler_params=params(),
        name="leaving",
    )(src, *x_slots, keys, scales, spread_four, g_state, total)


def scan_kernel(back_ref, part_ref, after_ref, out_ref):
    back = back_ref[0]
    head = lax.broadcasted_iota(jnp.int32, (EXTRA, WIDTH), 0)
    lane = lax.broadcasted_iota(jnp.int32, (EXTRA, WIDTH), 1)
    spread_one = ((head < 2 * HEADS) & (lane // HEAD_DIM == head % HEADS)).astype(BF16)
    decays_in = part_ref[:, :, WIDTH:].reshape(OWNERS * 16, EXTRA)
    decay_ref = dot(decays_in, spread_one).reshape(OWNERS, 16, WIDTH)
    order = [jnp.where(back == 1, OWNERS - 1 - k, k) for k in range(OWNERS)]
    held = jnp.zeros((16, WIDTH), F32)
    for k, at in enumerate(order):
        out_ref[at] = held.astype(BF16)
        decay = jnp.where(back == 1, decay_ref[OWNERS - 1 - k], decay_ref[k])
        held = decay * held + part_ref[at, :, 0:WIDTH].astype(F32)


def scan_owners(back, parts, after):
    return pl.pallas_call(
        scan_kernel,
        in_specs=[SMEM, WHOLE, ANY],
        out_specs=WHOLE,
        out_shape=jax.ShapeDtypeStruct((OWNERS, 16, WIDTH), BF16),
        compiler_params=params(),
        name="scan_owners",
    )(back, parts, after)


def finish_kernel(b_ref, c_ref, ya_ref, yb_ref, g_ref, enter_ref, scale_ref, spread_ref, y_out, g_out):
    rows = RUN * PIECE
    b, c = b_ref[...].reshape(rows, STATE), c_ref[...].reshape(rows, STATE)
    scales = scale_ref[...].reshape(rows, PIECE)
    for group in range(WIDTH // GROUP):
        cols = slice(group * GROUP, (group + 1) * GROUP)
        y_off = dot(scales, spread_ref[BEFORE, :, cols]) * dot(c, enter_ref[0:STATE, cols])
        start = group % 2 * GROUP
        y = (ya_ref if group < 2 else yb_ref)[:, :, start : start + GROUP].reshape(rows, GROUP)
        y_out[:, cols] = (y + y_off).astype(BF16)
        g_off = dot(scales, spread_ref[AFTER, :, cols]) * dot(b, enter_ref[STATE:, cols])
        g_out[:, cols] = (g_ref[:, :, cols].reshape(rows, GROUP) + g_off).astype(BF16)


def finish(b, c, y_a, y_b, g_local, enter, scales, spread_four):
    pieces = scales.shape[0]
    out = jax.ShapeDtypeStruct((pieces * PIECE, WIDTH), BF16)
    square = pl.BlockSpec((RUN, PIECE, PIECE), lambda k: (k, 0, 0))
    half = pl.BlockSpec((RUN, PIECE, HALF), lambda k: (k, 0, 0))
    wide = pl.BlockSpec((RUN, PIECE, WIDTH), lambda k: (k, 0, 0))
    return pl.pallas_call(
        finish_kernel,
        grid=(pieces // RUN,),
        in_specs=[
            square,
            square,
            half,
            half,
            wide,
            pl.BlockSpec((2 * STATE, WIDTH), lambda k: (0, 0)),
            square,
            pl.BlockSpec(spread_four.shape, lambda k: (0, 0, 0)),
        ],
        out_specs=[pl.BlockSpec((RUN * PIECE, WIDTH), lambda k: (k, 0))] * 2,
        out_shape=[out, out],
        compiler_params=params(),
        name="finish",
    )(b, c, y_a, y_b, g_local, enter, scales, spread_four)


def ranks(dest):
    owner = dest // OWNERS
    here = lax.broadcasted_iota(jnp.int32, (OWNERS, OWNERS), 0)
    other = lax.broadcasted_iota(jnp.int32, (OWNERS, OWNERS), 1)
    same = (owner[..., None, :] == owner[..., :, None]) & (other < here)
    return jnp.sum(same.astype(jnp.int32), axis=-1)


def to_owners(value):
    return lax.all_to_all(value, "ctx", split_axis=0, concat_axis=0, tiled=True)


def body(
    x_rows, b_rows, c_rows, dt_rows, destination, doc_start, a_log, dt_bias, d_skip, cotangent
):
    head = lax.axis_index("head")
    me = lax.axis_index("ctx")
    dest_heads = jnp.stack([partner(head, s) for s in SHIFTS]).astype(jnp.int32)
    origin = jnp.stack([source(head, s) for s in SHIFTS] + [head]).astype(jnp.int32)
    send_slot = destination // OWNERS * 2 + ranks(destination)

    small = gather_small(b_rows, c_rows, dt_rows)
    small = lax.all_to_all(small, "head", split_axis=0, concat_axis=0, tiled=True)
    cuts = [cut(half, dest_heads, x_rows) for half in range(2)]
    arrived = []
    for half in range(2):
        arrived.append([])
        for shift, piece in zip(SHIFTS, cuts[half]):
            pairs = [(h, partner(h, shift)) for h in range(PEERS)]
            arrived[half].append(lax.ppermute(piece, "head", pairs))
    small = small.reshape(OWNERS, SMALL_ROWS, STATE)
    small = pack_small(send_slot, destination % OWNERS, small, arrived[0][:EARLY])
    small = to_owners(small)

    pieces = destination.shape[0]
    seg = jnp.cumsum(doc_start.reshape(pieces, PIECE), axis=1).astype(F32)[:, None, :]
    bias, alog = dt_bias.reshape(HEADS, 1), a_log.reshape(HEADS, 1)
    skip = jnp.repeat(d_skip, HEAD_DIM).reshape(1, WIDTH)
    spread_four = spread(4)
    first = [seg, bias, alog, skip, spread_four, cuts[1][0]]
    x_a = pack_x(0, send_slot, origin, x_rows, arrived[0], first)
    x_a = to_owners(x_a)

    src = find_source(small)
    b, c, bt, ct, rows, cols, scales, ends, total = decays(src, small, seg, bias, alog)
    local = (rows, cols, scales, ends, spread_four, skip)
    g_state = leaving_gradient(ct, cotangent, scales, spread_four)
    g_local = backward_local(src, b, ct, cotangent, local, g_state)

    x_b = pack_x(1, send_slot, origin, x_rows, arrived[1], [g_state])
    x_slots = [x_a, to_owners(hold(x_b, [g_local]))]
    parts = leaving(src, x_slots, bt, scales, spread_four, g_state, total)
    y_a = forward_local(0, src, c, bt, x_slots, local, parts)
    back = (me >= OWNERS // 2).astype(jnp.int32).reshape(1)
    enter = scan_owners(back, to_owners(parts), y_a)
    y_b = forward_local(1, src, c, bt, x_slots, local, enter)
    enter = to_owners(enter).reshape(2 * STATE, WIDTH)
    return tuple(finish(b, c, y_a, y_b, g_local, enter, scales, spread_four))


def solution(mesh):
    in_specs = (
        P(("ctx", "head"), None),
        P(("ctx", "head"), None),
        P(("ctx", "head"), None),
        P(("ctx", "head"), None),
        P("ctx"),
        P("ctx"),
        P("head"),
        P("head"),
        P("head"),
        P("ctx", "head"),
    )
    out_specs = (P("ctx", "head"), P("ctx", "head"))
    return jax.shard_map(body, mesh=mesh, in_specs=in_specs, out_specs=out_specs, check_vma=False)
```

```python
from functools import partial

import jax
import jax.numpy as jnp
from jax import lax
from jax.experimental import pallas as pl
from jax.experimental.pallas import tpu as pltpu
from jax.sharding import PartitionSpec as P

OWNERS = 16
PEERS = 8
PIECE = 128
STATE = 128
HEADS = 16
HEAD_DIM = 64
WIDTH = HEADS * HEAD_DIM
HALF = WIDTH // 2
SMALL_ROWS = 2 * PIECE + HEADS
TAG_ROWS = 16
SENT_ROWS = SMALL_ROWS + TAG_ROWS
EXTRA = 128
LOG2E = 1.4426950408889634
F32 = jnp.float32
BF16 = jnp.bfloat16
ANY = pl.BlockSpec(memory_space=pl.ANY)
WHOLE = pl.BlockSpec(memory_space=pltpu.VMEM)
SMEM = pl.BlockSpec(memory_space=pltpu.SMEM)
EARLY = 2
SHIFTS = [(1, 0), (3, 0), (1, 1), (3, 1), (2, 0), (2, 1), (0, 1)]


def params(mib=56):
    return pltpu.CompilerParams(vmem_limit_bytes=mib * 1024 * 1024)


def partner(head, shift):
    return (head // 2 + shift[0]) % 4 * 2 + (head % 2 + shift[1]) % 2


def source(head, shift):
    return (head // 2 + 4 - shift[0]) % 4 * 2 + (head % 2 + shift[1]) % 2


def run_copies(copies):
    for copy in copies:
        copy.start()
    for copy in copies:
        copy.wait()


def gather_small_kernel(b_ref, c_ref, dt_ref, out_ref, turned, sems):
    copies = []
    for r in range(2):
        rows = pl.ds(r * PIECE, PIECE)
        for g in range(PEERS):
            cols = pl.ds(g * STATE, STATE)
            for kind, ref in enumerate((b_ref, c_ref)):
                copies.append(
                    pltpu.make_async_copy(
                        ref.at[rows, cols],
                        out_ref.at[g, r, pl.ds(kind * PIECE, PIECE), :],
                        sems.at[len(copies)],
                    )
                )
    for copy in copies:
        copy.start()
    last = []
    for r in range(2):
        dt_t = dt_ref[r * PIECE : (r + 1) * PIECE, :].astype(F32).T.astype(BF16)
        for g in range(PEERS):
            turned[g, r] = dt_t[g * HEADS : (g + 1) * HEADS, :]
    last = pltpu.make_async_copy(
        turned, out_ref.at[:, :, pl.ds(2 * PIECE, HEADS), :], sems.at[len(copies)]
    )
    last.start()
    for copy in copies + [last]:
        copy.wait()


def gather_small(b_rows, c_rows, dt_rows):
    return pl.pallas_call(
        gather_small_kernel,
        in_specs=[WHOLE, WHOLE, WHOLE],
        out_specs=ANY,
        out_shape=jax.ShapeDtypeStruct((PEERS, 2, SMALL_ROWS, STATE), BF16),
        scratch_shapes=[
            pltpu.VMEM((PEERS, 2, HEADS, PIECE), BF16),
            pltpu.SemaphoreType.DMA((4 * PEERS + 1,)),
        ],
        compiler_params=params(),
        name="gather_small",
    )(b_rows, c_rows, dt_rows)


def pack_small_kernel(slot_ref, place_ref, in_ref, *rest):
    out_ref, tags, sems = rest[-3:]
    copies = [
        pltpu.make_async_copy(
            in_ref.at[j], out_ref.at[slot_ref[j], pl.ds(0, SMALL_ROWS), :], sems.at[j]
        )
        for j in range(OWNERS)
    ]
    for copy in copies:
        copy.start()
    tags[...] = jnp.full(tags.shape, -1.0, BF16)
    for j in range(OWNERS):
        place = place_ref[j].astype(F32)
        tags[slot_ref[j]] = jnp.full(tags.shape[1:], place, F32).astype(BF16)
    last = pltpu.make_async_copy(
        tags, out_ref.at[:, pl.ds(SMALL_ROWS, TAG_ROWS), :], sems.at[OWNERS]
    )
    last.start()
    for copy in copies + [last]:
        copy.wait()


def pack_small(slot, place, pieces, after):
    return pl.pallas_call(
        pack_small_kernel,
        in_specs=[SMEM, SMEM, WHOLE] + [ANY] * len(after),
        out_specs=ANY,
        out_shape=jax.ShapeDtypeStruct((2 * OWNERS, SENT_ROWS, STATE), BF16),
        scratch_shapes=[
            pltpu.VMEM((2 * OWNERS, TAG_ROWS, STATE), BF16),
            pltpu.SemaphoreType.DMA((OWNERS + 1,)),
        ],
        compiler_params=params(),
        name="pack_small",
    )(slot, place, pieces, *after)


def find_source_kernel(small_ref, out_ref, tags, sem):
    copy = pltpu.make_async_copy(
        small_ref.at[:, pl.ds(SMALL_ROWS, TAG_ROWS), :], tags, sem.at[0]
    )
    copy.start()
    copy.wait()
    slot = lax.broadcasted_iota(jnp.int32, tags.shape, 0).astype(F32)
    place = lax.broadcasted_iota(jnp.int32, tags.shape, 2).astype(F32)
    found = jnp.where(tags[...].astype(F32) == place, slot, 0.0)
    out_ref[...] = jnp.sum(found, axis=0)[0:1].astype(jnp.int32)


def find_source(small):
    return pl.pallas_call(
        find_source_kernel,
        in_specs=[ANY],
        out_specs=pl.BlockSpec(memory_space=pltpu.VMEM),
        out_shape=jax.ShapeDtypeStruct((1, STATE), jnp.int32),
        scratch_shapes=[
            pltpu.VMEM((2 * OWNERS, TAG_ROWS, STATE), BF16),
            pltpu.SemaphoreType.DMA((1,)),
        ],
        compiler_params=params(20),
        name="find_source",
    )(small)


def cut_kernel(half, dest_ref, x_ref, *rest):
    count = len(SHIFTS)
    outs, (held, sems) = rest[:count], rest[count:]
    ins, copies = [], []
    for i in range(count):
        at = pl.multiple_of(dest_ref[i] * WIDTH + half * HALF, HALF)
        ins.append(pltpu.make_async_copy(x_ref.at[:, pl.ds(at, HALF)], held.at[i], sems.at[0, i]))
        copies.append(pltpu.make_async_copy(held.at[i], outs[i], sems.at[1, i]))
    for copy in ins:
        copy.start()
    for i in range(count):
        ins[i].wait()
        copies[i].start()
    for copy in copies:
        copy.wait()


def cut(half, dest, x_rows):
    count = len(SHIFTS)
    shape = (x_rows.shape[0], HALF)
    return pl.pallas_call(
        partial(cut_kernel, half),
        in_specs=[SMEM, ANY],
        out_specs=[ANY] * count,
        out_shape=[jax.ShapeDtypeStruct(shape, BF16)] * count,
        scratch_shapes=[
            pltpu.VMEM((count,) + shape, BF16),
            pltpu.SemaphoreType.DMA((2, count)),
        ],
        compiler_params=params(),
        name="cut",
    )(dest, x_rows)


def pack_x_kernel(half, slot_ref, from_ref, x_ref, *rest):
    arrived, (out_ref, held, sems) = rest[: len(SHIFTS)], rest[-3:]
    count = len(arrived)
    at = pl.multiple_of(from_ref[count] * WIDTH + half * HALF, HALF)
    ins, copies = [], []
    for i in range(count + 1):
        for r in range(2):
            n = 2 * i + r
            slot = slot_ref[from_ref[i] * 2 + r]
            rows = pl.ds(r * PIECE, PIECE)
            piece = arrived[i].at[rows, :] if i < count else x_ref.at[rows, pl.ds(at, HALF)]
            ins.append(pltpu.make_async_copy(piece, held.at[n], sems.at[0, n]))
            copies.append(pltpu.make_async_copy(held.at[n], out_ref.at[slot], sems.at[1, n]))
    for copy in ins:
        copy.start()
    for n, copy in enumerate(ins):
        copy.wait()
        copies[n].start()
    for copy in copies:
        copy.wait()


def pack_x(half, slot, origin, x_rows, arrived, after):
    return pl.pallas_call(
        partial(pack_x_kernel, half),
        in_specs=[SMEM, SMEM] + [ANY] * (1 + len(arrived) + len(after)),
        out_specs=ANY,
        out_shape=jax.ShapeDtypeStruct((2 * OWNERS, PIECE, HALF), BF16),
        scratch_shapes=[
            pltpu.VMEM((2 * PEERS, PIECE, HALF), BF16),
            pltpu.SemaphoreType.DMA((2, 2 * PEERS)),
        ],
        compiler_params=params(),
        name="pack_x",
    )(slot, origin, x_rows, *arrived, *after)


def hold_kernel(value_ref, *rest):
    del value_ref, rest


def hold(value, after):
    return pl.pallas_call(
        hold_kernel,
        in_specs=[ANY] * (1 + len(after)),
        out_specs=ANY,
        out_shape=jax.ShapeDtypeStruct(value.shape, value.dtype),
        input_output_aliases={0: 0},
        compiler_params=params(),
        name="hold",
    )(value, *after)


def split_two(value):
    high = value.astype(BF16)
    return high, (value - high.astype(F32)).astype(BF16)


def softplus(value):
    small = jnp.exp(-jnp.abs(value))
    series = small * (1.0 - small * (0.5 - small * (1.0 / 3.0 - small * 0.25)))
    return jnp.maximum(value, 0.0) + jnp.where(small < 1e-2, series, jnp.log(1.0 + small))


def decay_kernel(src_ref, small_ref, seg_ref, bias_ref, alog_ref, *rest):
    b_ref, c_ref, bt_ref, ct_ref, rows_ref, cols_ref, scale_ref, ends_ref, total_ref, dt_ref, sems = rest
    pieces = seg_ref.shape[0]
    copies = []
    for k in range(pieces):
        for at, to in enumerate((dt_ref, b_ref, c_ref)):
            start, size = ((2 * PIECE, HEADS), (0, PIECE), (PIECE, PIECE))[at]
            rows = small_ref.at[src_ref[0, k], pl.ds(start, size), :]
            copies.append(pltpu.make_async_copy(rows, to.at[k], sems.at[at, k]))
    for copy in copies:
        copy.start()
    for copy in copies:
        copy.wait()
    step_all = softplus(dt_ref[...].astype(F32) + bias_ref[...][None])
    rate_all = -step_all * (jnp.exp(alog_ref[...]) * LOG2E)[None]
    up_to = (
        lax.broadcasted_iota(jnp.int32, (PIECE, PIECE), 0)
        <= lax.broadcasted_iota(jnp.int32, (PIECE, PIECE), 1)
    ).astype(F32)
    log_all = jnp.dot(
        rate_all.reshape(pieces * HEADS, PIECE),
        up_to,
        precision=lax.Precision.HIGHEST,
        preferred_element_type=F32,
    ).reshape(pieces, HEADS, PIECE)
    ends = [log_all[k, :, PIECE - 1 :] for k in range(pieces)]
    starts = [seg_ref[k, :, PIECE - 1 :] for k in range(pieces)]
    none = jnp.zeros((1, 1), F32)
    log_before, starts_before = [jnp.zeros((HEADS, 1), F32)], [none]
    log_after, starts_after = [jnp.zeros((HEADS, 1), F32)], [none]
    for k in range(pieces):
        log_before.append(log_before[-1] + ends[k])
        starts_before.append(starts_before[-1] + starts[k])
        log_after.append(log_after[-1] + ends[pieces - 1 - k])
        starts_after.append(starts_after[-1] + starts[pieces - 1 - k])
    rest_rows = jnp.zeros((PIECE - 3 * HEADS - 1, PIECE), F32)
    head = lax.broadcasted_iota(jnp.int32, (HEADS, WIDTH), 0)
    lane = lax.broadcasted_iota(jnp.int32, (HEADS, WIDTH), 1)
    spread_one = (lane // HEAD_DIM == head).astype(BF16)
    for k in range(pieces):
        log, step, seg = log_all[k], step_all[k], seg_ref[k]
        shifted = log - jnp.log(step) * LOG2E
        rows = jnp.concatenate([log, shifted, step, seg, rest_rows], axis=0)
        rows_ref[k] = rows[0:ROW_COUNT]
        cols_ref[k] = rows.T
        bt_ref[k] = b_ref[k].astype(F32).T.astype(BF16)
        ct_ref[k] = c_ref[k].astype(F32).T.astype(BF16)
        none_yet = (seg == 0.0).astype(F32)
        none_left = (seg == starts[k]).astype(F32)
        left = pieces - 1 - k
        entry = jnp.exp2(log) * none_yet
        step_exit = step * (jnp.exp2(ends[k] - log) * none_left)
        no_before = none_yet * (starts_before[k] == 0.0).astype(F32)
        before = jnp.exp2(log_before[k] + log) * no_before
        no_after = none_left * (starts_after[left] == 0.0).astype(F32)
        after = step * (jnp.exp2(log_after[left] + (ends[k] - log)) * no_after)
        parts = []
        for value in (entry, step_exit, before, after):
            high = value.astype(BF16).astype(F32)
            parts += [high, value - high]
        scale_ref[k] = jnp.concatenate(parts, axis=0).T.astype(BF16)
        decay = jnp.exp2(ends[k]) * (starts[k] == 0.0).astype(F32)
        high, low = split_two(jnp.broadcast_to(decay, (HEADS, PIECE)))
        ends_ref[k] = (over_first(high, spread_one) + over_first(low, spread_one))[0:8]
    total = jnp.exp2(log_before[-1]) * (starts_before[-1] == 0.0).astype(F32)
    total = jnp.broadcast_to(total, (HEADS, PIECE))
    high = total.astype(BF16).astype(F32)
    blank = jnp.zeros((PIECE - 2 * HEADS, PIECE), F32)
    total_ref[...] = jnp.concatenate([high, total - high, blank], axis=0).T[0:16].astype(BF16)


ROW_COUNT = 56
SEG = 3 * HEADS
ENTRY, STEP_EXIT, BEFORE, AFTER = range(4)
GROUP = 256
RUN = 4


def decays(src, small, seg, bias, alog):
    pieces = seg.shape[0]
    square = (pieces, PIECE, PIECE)
    return pl.pallas_call(
        decay_kernel,
        in_specs=[SMEM, ANY, WHOLE, WHOLE, WHOLE],
        out_specs=[WHOLE] * 9,
        out_shape=[
            jax.ShapeDtypeStruct(square, BF16),
            jax.ShapeDtypeStruct(square, BF16),
            jax.ShapeDtypeStruct(square, BF16),
            jax.ShapeDtypeStruct(square, BF16),
            jax.ShapeDtypeStruct((pieces, ROW_COUNT, PIECE), F32),
            jax.ShapeDtypeStruct(square, F32),
            jax.ShapeDtypeStruct(square, BF16),
            jax.ShapeDtypeStruct((pieces, 8, WIDTH), F32),
            jax.ShapeDtypeStruct((16, EXTRA), BF16),
        ],
        scratch_shapes=[
            pltpu.VMEM((pieces, HEADS, PIECE), BF16),
            pltpu.SemaphoreType.DMA((3, pieces)),
        ],
        compiler_params=params(),
        name="decays",
    )(src, small, seg, bias, alog)


def spread(kinds):
    shape = (kinds, kinds * 2 * HEADS, WIDTH)
    rows = lax.broadcasted_iota(jnp.int32, shape, 1)
    kind = lax.broadcasted_iota(jnp.int32, shape, 0)
    head = lax.broadcasted_iota(jnp.int32, shape, 2) // HEAD_DIM
    return ((rows // (2 * HEADS) == kind) & (rows % HEADS == head)).astype(BF16)


def over_first(left, right):
    return lax.dot_general(left, right, (((0,), (0,)), ((), ())), preferred_element_type=F32)


def dot(left, right):
    return jnp.dot(left, right, preferred_element_type=F32)


def two_heads(weights, values):
    lane = lax.broadcasted_iota(jnp.int32, values.shape, 1)
    zero = jnp.zeros_like(values)
    stacked = jnp.concatenate(
        [jnp.where(lane < HEAD_DIM, values, zero), jnp.where(lane < HEAD_DIM, zero, values)], axis=0
    )
    return dot(jnp.concatenate(weights, axis=1), stacked)


def local_piece(forward, first, r, left, turned, values_of, rows_ref, cols_ref, scale_ref, ends_ref, spread_ref, skip_ref, out_ref, state):
    scales, by_token = scale_ref[r], cols_ref[r]
    row = lax.broadcasted_iota(jnp.int32, (PIECE, PIECE), 0)
    col = lax.broadcasted_iota(jnp.int32, (PIECE, PIECE), 1)
    same = by_token[:, SEG : SEG + 1] == rows_ref[r, SEG : SEG + 1, :]
    reach = (col <= row) if forward else (col >= row)
    scores = jnp.where(reach & same, dot(left, turned), 0.0)
    into, out_of = (ENTRY, STEP_EXIT) if forward else (STEP_EXIT, ENTRY)
    for group in range(out_ref.shape[2] // GROUP):
        cols = slice(group * GROUP, (group + 1) * GROUP)
        values = values_of(group)
        near = []
        for pair in range(2):
            weights = []
            for head in (first + 4 * group + 2 * pair, first + 4 * group + 2 * pair + 1):
                if forward:
                    gap = by_token[:, head : head + 1] - rows_ref[r, HEADS + head : HEADS + head + 1, :]
                else:
                    gap = rows_ref[r, head : head + 1, :] - by_token[:, head : head + 1]
                weights.append((scores * jnp.exp2(jnp.minimum(gap, 8.0))).astype(BF16))
            part = two_heads(weights, values[:, pair * 128 : (pair + 1) * 128])
            if not forward:
                at = 2 * HEADS + head
                lane = lax.broadcasted_iota(jnp.int32, part.shape, 1)
                part *= jnp.where(lane < HEAD_DIM, by_token[:, at - 1 : at], by_token[:, at : at + 1])
            near.append(part)
        wide = values.astype(F32)
        held = state[:, cols]
        out = jnp.concatenate(near, axis=1) + skip_ref[:, cols] * wide
        out += dot(scales, spread_ref[into, :, cols]) * dot(left, held.astype(BF16))
        out_ref[r, :, cols] = out.astype(BF16)
        scaled = (wide * dot(scales, spread_ref[out_of, :, cols])).astype(BF16)
        state[:, cols] = ends_ref[r, 0:1, cols] * held + dot(turned, scaled)


def forward_kernel(half, c_ref, bt_ref, *rest):
    x_refs, (after_ref, out_ref, state) = rest[:RUN], rest[-3:]

    @pl.when(pl.program_id(0) == 0)
    def _():
        state[...] = jnp.zeros_like(state)

    for r in range(RUN):

        def values_of(group):
            return x_refs[r][0, :, group * GROUP : (group + 1) * GROUP]

        local_piece(
            True, half * HEADS // 2, r, c_ref[r], bt_ref[r], values_of, *rest[RUN:-3], out_ref, state
        )


def backward_kernel(b_ref, ct_ref, cot_ref, *rest):
    after_ref, out_ref, state = rest[-3:]

    @pl.when(pl.program_id(0) == 0)
    def _():
        state[...] = jnp.zeros_like(state)

    for r in reversed(range(RUN)):

        def values_of(group):
            return cot_ref[r * PIECE : (r + 1) * PIECE, group * GROUP : (group + 1) * GROUP]

        local_piece(False, 0, r, b_ref[r], ct_ref[r], values_of, *rest[:-3], out_ref, state)


def local_call(kernel, place, width, half, firsts, specs, values, src, local, after, name):
    rows, cols, scales, ends, spread_four, skip = local
    pieces = rows.shape[0]
    at = lambda k, src: (place(k), 0, 0)
    square = pl.BlockSpec((RUN, PIECE, PIECE), at)
    return pl.pallas_call(
        skip_src(kernel),
        grid_spec=pltpu.PrefetchScalarGridSpec(
            num_scalar_prefetch=1,
            grid=(pieces // RUN,),
            in_specs=[
                square,
                square,
                *specs,
                pl.BlockSpec((RUN, ROW_COUNT, PIECE), at),
                square,
                square,
                pl.BlockSpec((RUN, 8, width), lambda k, src: (place(k), 0, half)),
                pl.BlockSpec((2, PIECE, width), lambda k, src: (0, 0, half)),
                pl.BlockSpec((1, width), lambda k, src: (0, half)),
                ANY,
            ],
            out_specs=pl.BlockSpec((RUN, PIECE, width), at),
            scratch_shapes=[pltpu.VMEM((STATE, width), F32)],
        ),
        out_shape=jax.ShapeDtypeStruct((pieces, PIECE, width), BF16),
        compiler_params=params(),
        name=name,
    )(src, *firsts, *values, rows, cols, scales, ends, spread_four, skip, after)


def skip_src(kernel):
    return lambda src_ref, *refs: kernel(*refs)


def forward_local(half, src, c, bt, x_slots, local, after):
    specs = [
        pl.BlockSpec((1, PIECE, HALF), lambda k, src, r=r: (src[0, RUN * k + r], 0, 0))
        for r in range(RUN)
    ]
    kernel = partial(forward_kernel, half)
    values = [x_slots[half]] * RUN
    return local_call(
        kernel, lambda k: k, HALF, half, [c, bt], specs, values, src, local, after, "forward_local"
    )


def backward_local(src, b, ct, cotangent, local, after):
    last = b.shape[0] // RUN - 1
    specs = [pl.BlockSpec((RUN * PIECE, WIDTH), lambda k, src: (last - k, 0))]
    place = lambda k: last - k
    return local_call(
        backward_kernel, place, WIDTH, 0, [b, ct], specs, [cotangent], src, local, after, "backward_local"
    )


def leaving_state(kind, keys_ref, v_all, scale_ref, spread_ref, state, wait):
    pieces = scale_ref.shape[0]
    for k in range(0, pieces, RUN):
        wait(k)
        scales = scale_ref[k : k + RUN].reshape(RUN * PIECE, PIECE)
        for group in range(WIDTH // GROUP):
            cols = slice(group * GROUP, (group + 1) * GROUP)
            scale = dot(scales, spread_ref[0, :, cols])
            values = v_all[k : k + RUN, :, cols].reshape(RUN * PIECE, GROUP)
            scaled = (values.astype(F32) * scale).astype(BF16)
            total = None if k == 0 else state[:, cols]
            for r in range(RUN):
                update = dot(keys_ref[k + r], scaled[r * PIECE : (r + 1) * PIECE])
                total = update if total is None else total + update
            state[:, cols] = total


def leaving_gradient_kernel(cot_ref, keys_ref, scale_ref, spread_ref, out_ref, v_all, state, sems):
    copies = [
        pltpu.make_async_copy(cot_ref.at[pl.ds(k * PIECE, PIECE), :], v_all.at[k], sems.at[k])
        for k in range(scale_ref.shape[0])
    ]
    for copy in copies:
        copy.start()

    def wait(k):
        for copy in copies[k : k + RUN]:
            copy.wait()

    leaving_state(BEFORE, keys_ref, v_all, scale_ref, spread_ref, state, wait)
    out_ref[...] = state[...].astype(BF16)


def kind_spec(kind):
    return pl.BlockSpec((1, PIECE, WIDTH), lambda i: (kind, 0, 0))


def leaving_gradient(keys, cotangent, scales, spread_four):
    pieces = scales.shape[0]
    return pl.pallas_call(
        leaving_gradient_kernel,
        grid=(1,),
        in_specs=[ANY, WHOLE, WHOLE, kind_spec(BEFORE)],
        out_specs=WHOLE,
        out_shape=jax.ShapeDtypeStruct((STATE, WIDTH), BF16),
        scratch_shapes=[
            pltpu.VMEM((pieces, PIECE, WIDTH), BF16),
            pltpu.VMEM((STATE, WIDTH), F32),
            pltpu.SemaphoreType.DMA((pieces,)),
        ],
        compiler_params=params(),
        name="leaving_gradient",
    )(cotangent, keys, scales, spread_four)


def leaving_kernel(src_ref, xa_ref, xb_ref, keys_ref, scale_ref, spread_ref, g_ref, total_ref, out_ref, v_all, state, sems):
    ins = []
    for k in range(scale_ref.shape[0]):
        for half, ref in enumerate((xa_ref, xb_ref)):
            to = v_all.at[k, :, pl.ds(half * HALF, HALF)]
            ins.append(pltpu.make_async_copy(ref.at[src_ref[0, k]], to, sems.at[half, k]))
    for copy in ins:
        copy.start()
    for part in range(OWNERS):
        out_ref[part, :, WIDTH:] = total_ref[...]
        if part >= 8:
            out_ref[part, :, 0:WIDTH] = g_ref[part % 8 * 16 : part % 8 * 16 + 16, :]

    def wait(k):
        for copy in ins[2 * k : 2 * (k + RUN)]:
            copy.wait()

    leaving_state(AFTER, keys_ref, v_all, scale_ref, spread_ref, state, wait)
    for part in range(8):
        out_ref[part, :, 0:WIDTH] = state[part * 16 : part * 16 + 16, :].astype(BF16)


def leaving(src, x_slots, keys, scales, spread_four, g_state, total):
    pieces = scales.shape[0]
    return pl.pallas_call(
        leaving_kernel,
        grid=(1,),
        in_specs=[SMEM, ANY, ANY, WHOLE, WHOLE, kind_spec(AFTER), WHOLE, WHOLE],
        out_specs=WHOLE,
        out_shape=jax.ShapeDtypeStruct((OWNERS, 16, WIDTH + EXTRA), BF16),
        scratch_shapes=[
            pltpu.VMEM((pieces, PIECE, WIDTH), BF16),
            pltpu.VMEM((STATE, WIDTH), F32),
            pltpu.SemaphoreType.DMA((2, pieces)),
        ],
        compiler_params=params(),
        name="leaving",
    )(src, *x_slots, keys, scales, spread_four, g_state, total)


def scan_kernel(back_ref, part_ref, after_ref, out_ref):
    back = back_ref[0]
    head = lax.broadcasted_iota(jnp.int32, (EXTRA, WIDTH), 0)
    lane = lax.broadcasted_iota(jnp.int32, (EXTRA, WIDTH), 1)
    spread_one = ((head < 2 * HEADS) & (lane // HEAD_DIM == head % HEADS)).astype(BF16)
    decays_in = part_ref[:, :, WIDTH:].reshape(OWNERS * 16, EXTRA)
    decay_ref = dot(decays_in, spread_one).reshape(OWNERS, 16, WIDTH)
    order = [jnp.where(back == 1, OWNERS - 1 - k, k) for k in range(OWNERS)]
    held = jnp.zeros((16, WIDTH), F32)
    for k, at in enumerate(order):
        out_ref[at] = held.astype(BF16)
        decay = jnp.where(back == 1, decay_ref[OWNERS - 1 - k], decay_ref[k])
        held = decay * held + part_ref[at, :, 0:WIDTH].astype(F32)


def scan_owners(back, parts, after):
    return pl.pallas_call(
        scan_kernel,
        in_specs=[SMEM, WHOLE, ANY],
        out_specs=WHOLE,
        out_shape=jax.ShapeDtypeStruct((OWNERS, 16, WIDTH), BF16),
        compiler_params=params(),
        name="scan_owners",
    )(back, parts, after)


def finish_kernel(b_ref, c_ref, ya_ref, yb_ref, g_ref, enter_ref, scale_ref, spread_ref, y_out, g_out):
    rows = RUN * PIECE
    b, c = b_ref[...].reshape(rows, STATE), c_ref[...].reshape(rows, STATE)
    scales = scale_ref[...].reshape(rows, PIECE)
    for group in range(WIDTH // GROUP):
        cols = slice(group * GROUP, (group + 1) * GROUP)
        y_off = dot(scales, spread_ref[BEFORE - 2, :, cols]) * dot(c, enter_ref[0:STATE, cols])
        start = group % 2 * GROUP
        y = (ya_ref if group < 2 else yb_ref)[:, :, start : start + GROUP].reshape(rows, GROUP)
        y_out[:, cols] = (y + y_off).astype(BF16)
        g_off = dot(scales, spread_ref[AFTER - 2, :, cols]) * dot(b, enter_ref[STATE:, cols])
        g_out[:, cols] = (g_ref[:, :, cols].reshape(rows, GROUP) + g_off).astype(BF16)


def finish(b, c, y_a, y_b, g_local, enter, scales, spread_four):
    pieces = scales.shape[0]
    out = jax.ShapeDtypeStruct((pieces * PIECE, WIDTH), BF16)
    square = pl.BlockSpec((RUN, PIECE, PIECE), lambda k: (k, 0, 0))
    half = pl.BlockSpec((RUN, PIECE, HALF), lambda k: (k, 0, 0))
    wide = pl.BlockSpec((RUN, PIECE, WIDTH), lambda k: (k, 0, 0))
    return pl.pallas_call(
        finish_kernel,
        grid=(pieces // RUN,),
        in_specs=[
            square,
            square,
            half,
            half,
            wide,
            pl.BlockSpec((2 * STATE, WIDTH), lambda k: (0, 0)),
            square,
            pl.BlockSpec((2, PIECE, WIDTH), lambda k: (1, 0, 0)),
        ],
        out_specs=[pl.BlockSpec((RUN * PIECE, WIDTH), lambda k: (k, 0))] * 2,
        out_shape=[out, out],
        compiler_params=params(),
        name="finish",
    )(b, c, y_a, y_b, g_local, enter, scales, spread_four)


def ranks(dest):
    owner = dest // OWNERS
    here = lax.broadcasted_iota(jnp.int32, (OWNERS, OWNERS), 0)
    other = lax.broadcasted_iota(jnp.int32, (OWNERS, OWNERS), 1)
    same = (owner[..., None, :] == owner[..., :, None]) & (other < here)
    return jnp.sum(same.astype(jnp.int32), axis=-1)


def to_owners(value):
    return lax.all_to_all(value, "ctx", split_axis=0, concat_axis=0, tiled=True)


def body(
    x_rows, b_rows, c_rows, dt_rows, destination, doc_start, a_log, dt_bias, d_skip, cotangent
):
    head = lax.axis_index("head")
    me = lax.axis_index("ctx")
    dest_heads = jnp.stack([partner(head, s) for s in SHIFTS]).astype(jnp.int32)
    origin = jnp.stack([source(head, s) for s in SHIFTS] + [head]).astype(jnp.int32)
    send_slot = destination // OWNERS * 2 + ranks(destination)

    small = gather_small(b_rows, c_rows, dt_rows)
    small = lax.all_to_all(small, "head", split_axis=0, concat_axis=0, tiled=True)
    cuts = [cut(half, dest_heads, x_rows) for half in range(2)]
    arrived = []
    for half in range(2):
        arrived.append([])
        for shift, piece in zip(SHIFTS, cuts[half]):
            pairs = [(h, partner(h, shift)) for h in range(PEERS)]
            arrived[half].append(lax.ppermute(piece, "head", pairs))
    small = small.reshape(OWNERS, SMALL_ROWS, STATE)
    small = pack_small(send_slot, destination % OWNERS, small, arrived[0][:EARLY])
    small = to_owners(small)

    pieces = destination.shape[0]
    seg = jnp.cumsum(doc_start.reshape(pieces, PIECE), axis=1).astype(F32)[:, None, :]
    bias, alog = dt_bias.reshape(HEADS, 1), a_log.reshape(HEADS, 1)
    skip = jnp.repeat(d_skip, HEAD_DIM).reshape(1, WIDTH)
    spread_four = spread(4)
    first = [seg, bias, alog, skip, spread_four, cuts[1][0]]
    x_a = pack_x(0, send_slot, origin, x_rows, arrived[0], first)
    x_a = to_owners(x_a)

    src = find_source(small)
    b, c, bt, ct, rows, cols, scales, ends, total = decays(src, small, seg, bias, alog)
    local = (rows, cols, scales, ends, spread_four, skip)
    g_state = leaving_gradient(ct, cotangent, scales, spread_four)
    g_local = backward_local(src, b, ct, cotangent, local, g_state)

    x_b = pack_x(1, send_slot, origin, x_rows, arrived[1], [g_state])
    x_slots = [x_a, to_owners(hold(x_b, [g_local]))]
    parts = leaving(src, x_slots, bt, scales, spread_four, g_state, total)
    y_a = forward_local(0, src, c, bt, x_slots, local, parts)
    back = (me >= OWNERS // 2).astype(jnp.int32).reshape(1)
    enter = scan_owners(back, to_owners(parts), y_a)
    y_b = forward_local(1, src, c, bt, x_slots, local, enter)
    enter = to_owners(enter).reshape(2 * STATE, WIDTH)
    return tuple(finish(b, c, y_a, y_b, g_local, enter, scales, spread_four))


def solution(mesh):
    in_specs = (
        P(("ctx", "head"), None),
        P(("ctx", "head"), None),
        P(("ctx", "head"), None),
        P(("ctx", "head"), None),
        P("ctx"),
        P("ctx"),
        P("head"),
        P("head"),
        P("head"),
        P("ctx", "head"),
    )
    out_specs = (P("ctx", "head"), P("ctx", "head"))
    return jax.shard_map(body, mesh=mesh, in_specs=in_specs, out_specs=out_specs, check_vma=False)
```

```python
from functools import partial

import jax
import jax.numpy as jnp
from jax import lax
from jax.experimental import pallas as pl
from jax.experimental.pallas import tpu as pltpu
from jax.sharding import PartitionSpec as P

OWNERS = 16
PEERS = 8
PIECE = 128
STATE = 128
HEADS = 16
HEAD_DIM = 64
WIDTH = HEADS * HEAD_DIM
HALF = WIDTH // 2
SMALL_ROWS = 2 * PIECE + HEADS
TAG_ROWS = 16
SENT_ROWS = SMALL_ROWS + TAG_ROWS
EXTRA = 128
LOG2E = 1.4426950408889634
F32 = jnp.float32
BF16 = jnp.bfloat16
ANY = pl.BlockSpec(memory_space=pl.ANY)
WHOLE = pl.BlockSpec(memory_space=pltpu.VMEM)
SMEM = pl.BlockSpec(memory_space=pltpu.SMEM)
EARLY = 2
SHIFTS = [(1, 0), (3, 0), (1, 1), (3, 1), (2, 0), (2, 1), (0, 1)]


def params(mib=56):
    return pltpu.CompilerParams(vmem_limit_bytes=mib * 1024 * 1024)


def partner(head, shift):
    return (head // 2 + shift[0]) % 4 * 2 + (head % 2 + shift[1]) % 2


def source(head, shift):
    return (head // 2 + 4 - shift[0]) % 4 * 2 + (head % 2 + shift[1]) % 2


def run_copies(copies):
    for copy in copies:
        copy.start()
    for copy in copies:
        copy.wait()


def gather_small_kernel(b_ref, c_ref, dt_ref, out_ref, turned, sems):
    copies = []
    for r in range(2):
        rows = pl.ds(r * PIECE, PIECE)
        for g in range(PEERS):
            cols = pl.ds(g * STATE, STATE)
            for kind, ref in enumerate((b_ref, c_ref)):
                copies.append(
                    pltpu.make_async_copy(
                        ref.at[rows, cols],
                        out_ref.at[g, r, pl.ds(kind * PIECE, PIECE), :],
                        sems.at[len(copies)],
                    )
                )
    for copy in copies:
        copy.start()
    last = []
    for r in range(2):
        dt_t = dt_ref[r * PIECE : (r + 1) * PIECE, :].astype(F32).T.astype(BF16)
        for g in range(PEERS):
            turned[g, r] = dt_t[g * HEADS : (g + 1) * HEADS, :]
    last = pltpu.make_async_copy(
        turned, out_ref.at[:, :, pl.ds(2 * PIECE, HEADS), :], sems.at[len(copies)]
    )
    last.start()
    for copy in copies + [last]:
        copy.wait()


def gather_small(b_rows, c_rows, dt_rows):
    return pl.pallas_call(
        gather_small_kernel,
        in_specs=[WHOLE, WHOLE, WHOLE],
        out_specs=ANY,
        out_shape=jax.ShapeDtypeStruct((PEERS, 2, SMALL_ROWS, STATE), BF16),
        scratch_shapes=[
            pltpu.VMEM((PEERS, 2, HEADS, PIECE), BF16),
            pltpu.SemaphoreType.DMA((4 * PEERS + 1,)),
        ],
        compiler_params=params(),
        name="gather_small",
    )(b_rows, c_rows, dt_rows)


def pack_small_kernel(slot_ref, place_ref, in_ref, *rest):
    out_ref, tags, sems = rest[-3:]
    copies = [
        pltpu.make_async_copy(
            in_ref.at[j], out_ref.at[slot_ref[j], pl.ds(0, SMALL_ROWS), :], sems.at[j]
        )
        for j in range(OWNERS)
    ]
    for copy in copies:
        copy.start()
    tags[...] = jnp.full(tags.shape, -1.0, BF16)
    for j in range(OWNERS):
        place = place_ref[j].astype(F32)
        tags[slot_ref[j]] = jnp.full(tags.shape[1:], place, F32).astype(BF16)
    last = pltpu.make_async_copy(
        tags, out_ref.at[:, pl.ds(SMALL_ROWS, TAG_ROWS), :], sems.at[OWNERS]
    )
    last.start()
    for copy in copies + [last]:
        copy.wait()


def pack_small(slot, place, pieces, after):
    return pl.pallas_call(
        pack_small_kernel,
        in_specs=[SMEM, SMEM, WHOLE] + [ANY] * len(after),
        out_specs=ANY,
        out_shape=pltpu.HBM((2 * OWNERS, SENT_ROWS, STATE), BF16),
        scratch_shapes=[
            pltpu.VMEM((2 * OWNERS, TAG_ROWS, STATE), BF16),
            pltpu.SemaphoreType.DMA((OWNERS + 1,)),
        ],
        compiler_params=params(20),
        name="pack_small",
    )(slot, place, pieces, *after)


def find_source_kernel(small_ref, out_ref, tags, sem):
    copy = pltpu.make_async_copy(
        small_ref.at[:, pl.ds(SMALL_ROWS, TAG_ROWS), :], tags, sem.at[0]
    )
    copy.start()
    copy.wait()
    slot = lax.broadcasted_iota(jnp.int32, tags.shape, 0).astype(F32)
    place = lax.broadcasted_iota(jnp.int32, tags.shape, 2).astype(F32)
    found = jnp.where(tags[...].astype(F32) == place, slot, 0.0)
    out_ref[...] = jnp.sum(found, axis=0)[0:1].astype(jnp.int32)


def find_source(small):
    return pl.pallas_call(
        find_source_kernel,
        in_specs=[ANY],
        out_specs=pl.BlockSpec(memory_space=pltpu.VMEM),
        out_shape=jax.ShapeDtypeStruct((1, STATE), jnp.int32),
        scratch_shapes=[
            pltpu.VMEM((2 * OWNERS, TAG_ROWS, STATE), BF16),
            pltpu.SemaphoreType.DMA((1,)),
        ],
        compiler_params=params(20),
        name="find_source",
    )(small)


def cut_kernel(half, dest_ref, x_ref, *rest):
    count = PEERS
    outs, (held, sems) = rest[:count], rest[count:]
    ins, copies = [], []
    for i in range(count):
        at = pl.multiple_of(dest_ref[i] * WIDTH + half * HALF, HALF)
        ins.append(pltpu.make_async_copy(x_ref.at[:, pl.ds(at, HALF)], held.at[i], sems.at[0, i]))
        copies.append(pltpu.make_async_copy(held.at[i], outs[i], sems.at[1, i]))
    for copy in ins:
        copy.start()
    for i in range(count):
        ins[i].wait()
        copies[i].start()
    for copy in copies:
        copy.wait()


def cut(half, dest, x_rows):
    count = PEERS
    shape = (x_rows.shape[0], HALF)
    return pl.pallas_call(
        partial(cut_kernel, half),
        in_specs=[SMEM, ANY],
        out_specs=[ANY] * count,
        out_shape=[jax.ShapeDtypeStruct(shape, BF16)] * count,
        scratch_shapes=[
            pltpu.VMEM((count,) + shape, BF16),
            pltpu.SemaphoreType.DMA((2, count)),
        ],
        compiler_params=params(),
        name="cut",
    )(dest, x_rows)


def pack_x_kernel(slot_ref, from_ref, *rest):
    arrived, (out_ref, held, sems) = rest[:PEERS], rest[-3:]
    ins, copies = [], []
    for i in range(PEERS):
        for r in range(2):
            n = 2 * i + r
            slot = slot_ref[from_ref[i] * 2 + r]
            rows = pl.ds(r * PIECE, PIECE)
            piece = arrived[i].at[rows, :]
            ins.append(pltpu.make_async_copy(piece, held.at[n], sems.at[0, n]))
            copies.append(pltpu.make_async_copy(held.at[n], out_ref.at[slot], sems.at[1, n]))
    for copy in ins:
        copy.start()
    for n, copy in enumerate(ins):
        copy.wait()
        copies[n].start()
    for copy in copies:
        copy.wait()


def pack_x(slot, origin, arrived, after):
    return pl.pallas_call(
        pack_x_kernel,
        in_specs=[SMEM, SMEM] + [ANY] * (len(arrived) + len(after)),
        out_specs=ANY,
        out_shape=pltpu.HBM((2 * OWNERS, PIECE, HALF), BF16),
        scratch_shapes=[
            pltpu.VMEM((2 * PEERS, PIECE, HALF), BF16),
            pltpu.SemaphoreType.DMA((2, 2 * PEERS)),
        ],
        compiler_params=params(20),
        name="pack_x",
    )(slot, origin, *arrived, *after)


def hold_kernel(value_ref, *rest):
    del value_ref, rest


def hold(value, after):
    return pl.pallas_call(
        hold_kernel,
        in_specs=[ANY] * (1 + len(after)),
        out_specs=ANY,
        out_shape=jax.ShapeDtypeStruct(value.shape, value.dtype),
        input_output_aliases={0: 0},
        compiler_params=params(),
        name="hold",
    )(value, *after)


def split_two(value):
    high = value.astype(BF16)
    return high, (value - high.astype(F32)).astype(BF16)


def softplus(value):
    small = jnp.exp(-jnp.abs(value))
    series = small * (1.0 - small * (0.5 - small * (1.0 / 3.0 - small * 0.25)))
    return jnp.maximum(value, 0.0) + jnp.where(small < 1e-2, series, jnp.log(1.0 + small))


def decay_kernel(src_ref, small_ref, seg_ref, bias_ref, alog_ref, *rest):
    b_ref, c_ref, bt_ref, ct_ref, rows_ref, cols_ref, scale_ref, ends_ref, total_ref, dt_ref, sems = rest
    pieces = seg_ref.shape[0]
    copies = []
    for k in range(pieces):
        for at, to in enumerate((dt_ref, b_ref, c_ref)):
            start, size = ((2 * PIECE, HEADS), (0, PIECE), (PIECE, PIECE))[at]
            rows = small_ref.at[src_ref[0, k], pl.ds(start, size), :]
            copies.append(pltpu.make_async_copy(rows, to.at[k], sems.at[at, k]))
    for copy in copies:
        copy.start()
    for copy in copies:
        copy.wait()
    step_all = softplus(dt_ref[...].astype(F32) + bias_ref[...][None])
    rate_all = -step_all * (jnp.exp(alog_ref[...]) * LOG2E)[None]
    up_to = (
        lax.broadcasted_iota(jnp.int32, (PIECE, PIECE), 0)
        <= lax.broadcasted_iota(jnp.int32, (PIECE, PIECE), 1)
    ).astype(F32)
    log_all = jnp.dot(
        rate_all.reshape(pieces * HEADS, PIECE),
        up_to,
        precision=lax.Precision.HIGHEST,
        preferred_element_type=F32,
    ).reshape(pieces, HEADS, PIECE)
    ends = [log_all[k, :, PIECE - 1 :] for k in range(pieces)]
    starts = [seg_ref[k, :, PIECE - 1 :] for k in range(pieces)]
    none = jnp.zeros((1, 1), F32)
    log_before, starts_before = [jnp.zeros((HEADS, 1), F32)], [none]
    log_after, starts_after = [jnp.zeros((HEADS, 1), F32)], [none]
    for k in range(pieces):
        log_before.append(log_before[-1] + ends[k])
        starts_before.append(starts_before[-1] + starts[k])
        log_after.append(log_after[-1] + ends[pieces - 1 - k])
        starts_after.append(starts_after[-1] + starts[pieces - 1 - k])
    rest_rows = jnp.zeros((PIECE - 3 * HEADS - 1, PIECE), F32)
    head = lax.broadcasted_iota(jnp.int32, (HEADS, WIDTH), 0)
    lane = lax.broadcasted_iota(jnp.int32, (HEADS, WIDTH), 1)
    spread_one = (lane // HEAD_DIM == head).astype(BF16)
    for k in range(pieces):
        log, step, seg = log_all[k], step_all[k], seg_ref[k]
        shifted = log - jnp.log(step) * LOG2E
        rows = jnp.concatenate([log, shifted, step, seg, rest_rows], axis=0)
        rows_ref[k] = rows[0:ROW_COUNT]
        cols_ref[k] = rows.T
        bt_ref[k] = b_ref[k].astype(F32).T.astype(BF16)
        ct_ref[k] = c_ref[k].astype(F32).T.astype(BF16)
        none_yet = (seg == 0.0).astype(F32)
        none_left = (seg == starts[k]).astype(F32)
        left = pieces - 1 - k
        entry = jnp.exp2(log) * none_yet
        step_exit = step * (jnp.exp2(ends[k] - log) * none_left)
        no_before = none_yet * (starts_before[k] == 0.0).astype(F32)
        before = jnp.exp2(log_before[k] + log) * no_before
        no_after = none_left * (starts_after[left] == 0.0).astype(F32)
        after = step * (jnp.exp2(log_after[left] + (ends[k] - log)) * no_after)
        parts = []
        for value in (entry, step_exit, before, after):
            high = value.astype(BF16).astype(F32)
            parts += [high, value - high]
        scale_ref[k] = jnp.concatenate(parts, axis=0).T.astype(BF16)
        decay = jnp.exp2(ends[k]) * (starts[k] == 0.0).astype(F32)
        high, low = split_two(jnp.broadcast_to(decay, (HEADS, PIECE)))
        ends_ref[k] = (over_first(high, spread_one) + over_first(low, spread_one))[0:8]
    total = jnp.exp2(log_before[-1]) * (starts_before[-1] == 0.0).astype(F32)
    total = jnp.broadcast_to(total, (HEADS, PIECE))
    high = total.astype(BF16).astype(F32)
    blank = jnp.zeros((PIECE - 2 * HEADS, PIECE), F32)
    total_ref[...] = jnp.concatenate([high, total - high, blank], axis=0).T[0:16].astype(BF16)


ROW_COUNT = 56
SEG = 3 * HEADS
ENTRY, STEP_EXIT, BEFORE, AFTER = range(4)
GROUP = 256
RUN = 4


def decays(src, small, seg, bias, alog):
    pieces = seg.shape[0]
    square = (pieces, PIECE, PIECE)
    return pl.pallas_call(
        decay_kernel,
        in_specs=[SMEM, ANY, WHOLE, WHOLE, WHOLE],
        out_specs=[WHOLE] * 9,
        out_shape=[
            jax.ShapeDtypeStruct(square, BF16),
            jax.ShapeDtypeStruct(square, BF16),
            jax.ShapeDtypeStruct(square, BF16),
            jax.ShapeDtypeStruct(square, BF16),
            jax.ShapeDtypeStruct((pieces, ROW_COUNT, PIECE), F32),
            jax.ShapeDtypeStruct(square, F32),
            jax.ShapeDtypeStruct(square, BF16),
            jax.ShapeDtypeStruct((pieces, 8, WIDTH), F32),
            jax.ShapeDtypeStruct((16, EXTRA), BF16),
        ],
        scratch_shapes=[
            pltpu.VMEM((pieces, HEADS, PIECE), BF16),
            pltpu.SemaphoreType.DMA((3, pieces)),
        ],
        compiler_params=params(),
        name="decays",
    )(src, small, seg, bias, alog)


def spread(kinds):
    shape = (kinds, kinds * 2 * HEADS, WIDTH)
    rows = lax.broadcasted_iota(jnp.int32, shape, 1)
    kind = lax.broadcasted_iota(jnp.int32, shape, 0)
    head = lax.broadcasted_iota(jnp.int32, shape, 2) // HEAD_DIM
    return ((rows // (2 * HEADS) == kind) & (rows % HEADS == head)).astype(BF16)


def over_first(left, right):
    return lax.dot_general(left, right, (((0,), (0,)), ((), ())), preferred_element_type=F32)


def dot(left, right):
    return jnp.dot(left, right, preferred_element_type=F32)


def two_heads(weights, values):
    lane = lax.broadcasted_iota(jnp.int32, values.shape, 1)
    zero = jnp.zeros_like(values)
    stacked = jnp.concatenate(
        [jnp.where(lane < HEAD_DIM, values, zero), jnp.where(lane < HEAD_DIM, zero, values)], axis=0
    )
    return dot(jnp.concatenate(weights, axis=1), stacked)


def local_piece(forward, first, r, left, turned, values_of, rows_ref, cols_ref, scale_ref, ends_ref, spread_ref, skip_ref, out_ref, state):
    scales, by_token = scale_ref[r], cols_ref[r]
    row = lax.broadcasted_iota(jnp.int32, (PIECE, PIECE), 0)
    col = lax.broadcasted_iota(jnp.int32, (PIECE, PIECE), 1)
    same = by_token[:, SEG : SEG + 1] == rows_ref[r, SEG : SEG + 1, :]
    reach = (col <= row) if forward else (col >= row)
    scores = jnp.where(reach & same, dot(left, turned), 0.0)
    into, out_of = (ENTRY, STEP_EXIT) if forward else (STEP_EXIT, ENTRY)
    for group in range(out_ref.shape[2] // GROUP):
        cols = slice(group * GROUP, (group + 1) * GROUP)
        values = values_of(group)
        near = []
        for pair in range(2):
            weights = []
            for head in (first + 4 * group + 2 * pair, first + 4 * group + 2 * pair + 1):
                if forward:
                    gap = by_token[:, head : head + 1] - rows_ref[r, HEADS + head : HEADS + head + 1, :]
                else:
                    gap = rows_ref[r, head : head + 1, :] - by_token[:, head : head + 1]
                weights.append((scores * jnp.exp2(jnp.minimum(gap, 8.0))).astype(BF16))
            part = two_heads(weights, values[:, pair * 128 : (pair + 1) * 128])
            if not forward:
                at = 2 * HEADS + head
                lane = lax.broadcasted_iota(jnp.int32, part.shape, 1)
                part *= jnp.where(lane < HEAD_DIM, by_token[:, at - 1 : at], by_token[:, at : at + 1])
            near.append(part)
        wide = values.astype(F32)
        held = state[:, cols]
        out = jnp.concatenate(near, axis=1) + skip_ref[:, cols] * wide
        out += dot(scales, spread_ref[into, :, cols]) * dot(left, held.astype(BF16))
        out_ref[r, :, cols] = out.astype(BF16)
        scaled = (wide * dot(scales, spread_ref[out_of, :, cols])).astype(BF16)
        state[:, cols] = ends_ref[r, 0:1, cols] * held + dot(turned, scaled)


def forward_kernel(half, c_ref, bt_ref, *rest):
    x_refs, (after_ref, out_ref, state) = rest[:RUN], rest[-3:]

    @pl.when(pl.program_id(0) == 0)
    def _():
        state[...] = jnp.zeros_like(state)

    for r in range(RUN):

        def values_of(group):
            return x_refs[r][0, :, group * GROUP : (group + 1) * GROUP]

        local_piece(
            True, half * HEADS // 2, r, c_ref[r], bt_ref[r], values_of, *rest[RUN:-3], out_ref, state
        )


def backward_kernel(b_ref, ct_ref, cot_ref, *rest):
    after_ref, out_ref, state = rest[-3:]

    @pl.when(pl.program_id(0) == 0)
    def _():
        state[...] = jnp.zeros_like(state)

    for r in reversed(range(RUN)):

        def values_of(group):
            return cot_ref[r * PIECE : (r + 1) * PIECE, group * GROUP : (group + 1) * GROUP]

        local_piece(False, 0, r, b_ref[r], ct_ref[r], values_of, *rest[:-3], out_ref, state)


def local_call(kernel, place, width, half, firsts, specs, values, src, local, after, name):
    rows, cols, scales, ends, spread_four, skip = local
    pieces = rows.shape[0]
    at = lambda k, src: (place(k), 0, 0)
    square = pl.BlockSpec((RUN, PIECE, PIECE), at)
    return pl.pallas_call(
        skip_src(kernel),
        grid_spec=pltpu.PrefetchScalarGridSpec(
            num_scalar_prefetch=1,
            grid=(pieces // RUN,),
            in_specs=[
                square,
                square,
                *specs,
                pl.BlockSpec((RUN, ROW_COUNT, PIECE), at),
                square,
                square,
                pl.BlockSpec((RUN, 8, width), lambda k, src: (place(k), 0, half)),
                pl.BlockSpec((2, PIECE, width), lambda k, src: (0, 0, half)),
                pl.BlockSpec((1, width), lambda k, src: (0, half)),
                ANY,
            ],
            out_specs=pl.BlockSpec((RUN, PIECE, width), at),
            scratch_shapes=[pltpu.VMEM((STATE, width), F32)],
        ),
        out_shape=jax.ShapeDtypeStruct((pieces, PIECE, width), BF16),
        compiler_params=params(),
        name=name,
    )(src, *firsts, *values, rows, cols, scales, ends, spread_four, skip, after)


def skip_src(kernel):
    return lambda src_ref, *refs: kernel(*refs)


def forward_local(half, src, c, bt, x_slots, local, after):
    specs = [
        pl.BlockSpec((1, PIECE, HALF), lambda k, src, r=r: (src[0, RUN * k + r], 0, 0))
        for r in range(RUN)
    ]
    kernel = partial(forward_kernel, half)
    values = [x_slots[half]] * RUN
    return local_call(
        kernel, lambda k: k, HALF, half, [c, bt], specs, values, src, local, after, "forward_local"
    )


def backward_local(src, b, ct, cotangent, local, after):
    last = b.shape[0] // RUN - 1
    specs = [pl.BlockSpec((RUN * PIECE, WIDTH), lambda k, src: (last - k, 0))]
    place = lambda k: last - k
    return local_call(
        backward_kernel, place, WIDTH, 0, [b, ct], specs, [cotangent], src, local, after, "backward_local"
    )


def leaving_state(kind, keys_ref, v_all, scale_ref, spread_ref, state, wait):
    pieces = scale_ref.shape[0]
    for k in range(0, pieces, RUN):
        wait(k)
        scales = scale_ref[k : k + RUN].reshape(RUN * PIECE, PIECE)
        for group in range(WIDTH // GROUP):
            cols = slice(group * GROUP, (group + 1) * GROUP)
            scale = dot(scales, spread_ref[0, :, cols])
            values = v_all[k : k + RUN, :, cols].reshape(RUN * PIECE, GROUP)
            scaled = (values.astype(F32) * scale).astype(BF16)
            total = None if k == 0 else state[:, cols]
            for r in range(RUN):
                update = dot(keys_ref[k + r], scaled[r * PIECE : (r + 1) * PIECE])
                total = update if total is None else total + update
            state[:, cols] = total


def leaving_gradient_kernel(cot_ref, keys_ref, scale_ref, spread_ref, out_ref, v_all, state, sems):
    copies = [
        pltpu.make_async_copy(cot_ref.at[pl.ds(k * PIECE, PIECE), :], v_all.at[k], sems.at[k])
        for k in range(scale_ref.shape[0])
    ]
    for copy in copies:
        copy.start()

    def wait(k):
        for copy in copies[k : k + RUN]:
            copy.wait()

    leaving_state(BEFORE, keys_ref, v_all, scale_ref, spread_ref, state, wait)
    out_ref[...] = state[...].astype(BF16)


def kind_spec(kind):
    return pl.BlockSpec((1, PIECE, WIDTH), lambda i: (kind, 0, 0))


def leaving_gradient(keys, cotangent, scales, spread_four):
    pieces = scales.shape[0]
    return pl.pallas_call(
        leaving_gradient_kernel,
        grid=(1,),
        in_specs=[ANY, WHOLE, WHOLE, kind_spec(BEFORE)],
        out_specs=WHOLE,
        out_shape=jax.ShapeDtypeStruct((STATE, WIDTH), BF16),
        scratch_shapes=[
            pltpu.VMEM((pieces, PIECE, WIDTH), BF16),
            pltpu.VMEM((STATE, WIDTH), F32),
            pltpu.SemaphoreType.DMA((pieces,)),
        ],
        compiler_params=params(),
        name="leaving_gradient",
    )(cotangent, keys, scales, spread_four)


def leaving_kernel(src_ref, xa_ref, xb_ref, keys_ref, scale_ref, spread_ref, g_ref, total_ref, out_ref, v_all, state, sems):
    ins = []
    for k in range(scale_ref.shape[0]):
        for half, ref in enumerate((xa_ref, xb_ref)):
            to = v_all.at[k, :, pl.ds(half * HALF, HALF)]
            ins.append(pltpu.make_async_copy(ref.at[src_ref[0, k]], to, sems.at[half, k]))
    for copy in ins:
        copy.start()
    for part in range(OWNERS):
        out_ref[part, :, WIDTH:] = total_ref[...]
        if part >= 8:
            out_ref[part, :, 0:WIDTH] = g_ref[part % 8 * 16 : part % 8 * 16 + 16, :]

    def wait(k):
        for copy in ins[2 * k : 2 * (k + RUN)]:
            copy.wait()

    leaving_state(AFTER, keys_ref, v_all, scale_ref, spread_ref, state, wait)
    for part in range(8):
        out_ref[part, :, 0:WIDTH] = state[part * 16 : part * 16 + 16, :].astype(BF16)


def leaving(src, x_slots, keys, scales, spread_four, g_state, total):
    pieces = scales.shape[0]
    return pl.pallas_call(
        leaving_kernel,
        grid=(1,),
        in_specs=[SMEM, ANY, ANY, WHOLE, WHOLE, kind_spec(AFTER), WHOLE, WHOLE],
        out_specs=WHOLE,
        out_shape=jax.ShapeDtypeStruct((OWNERS, 16, WIDTH + EXTRA), BF16),
        scratch_shapes=[
            pltpu.VMEM((pieces, PIECE, WIDTH), BF16),
            pltpu.VMEM((STATE, WIDTH), F32),
            pltpu.SemaphoreType.DMA((2, pieces)),
        ],
        compiler_params=params(),
        name="leaving",
    )(src, *x_slots, keys, scales, spread_four, g_state, total)


def scan_kernel(back_ref, part_ref, after_ref, out_ref):
    back = back_ref[0]
    head = lax.broadcasted_iota(jnp.int32, (EXTRA, WIDTH), 0)
    lane = lax.broadcasted_iota(jnp.int32, (EXTRA, WIDTH), 1)
    spread_one = ((head < 2 * HEADS) & (lane // HEAD_DIM == head % HEADS)).astype(BF16)
    decays_in = part_ref[:, :, WIDTH:].reshape(OWNERS * 16, EXTRA)
    decay_ref = dot(decays_in, spread_one).reshape(OWNERS, 16, WIDTH)
    order = [jnp.where(back == 1, OWNERS - 1 - k, k) for k in range(OWNERS)]
    held = jnp.zeros((16, WIDTH), F32)
    for k, at in enumerate(order):
        out_ref[at] = held.astype(BF16)
        decay = jnp.where(back == 1, decay_ref[OWNERS - 1 - k], decay_ref[k])
        held = decay * held + part_ref[at, :, 0:WIDTH].astype(F32)


def scan_owners(back, parts, after):
    return pl.pallas_call(
        scan_kernel,
        in_specs=[SMEM, WHOLE, ANY],
        out_specs=WHOLE,
        out_shape=jax.ShapeDtypeStruct((OWNERS, 16, WIDTH), BF16),
        compiler_params=params(),
        name="scan_owners",
    )(back, parts, after)


def finish_kernel(b_ref, c_ref, ya_ref, yb_ref, g_ref, enter_ref, scale_ref, spread_ref, y_out, g_out):
    rows = RUN * PIECE
    b, c = b_ref[...].reshape(rows, STATE), c_ref[...].reshape(rows, STATE)
    scales = scale_ref[...].reshape(rows, PIECE)
    for group in range(WIDTH // GROUP):
        cols = slice(group * GROUP, (group + 1) * GROUP)
        y_off = dot(scales, spread_ref[BEFORE - 2, :, cols]) * dot(c, enter_ref[0:STATE, cols])
        start = group % 2 * GROUP
        y = (ya_ref if group < 2 else yb_ref)[:, :, start : start + GROUP].reshape(rows, GROUP)
        y_out[:, cols] = (y + y_off).astype(BF16)
        g_off = dot(scales, spread_ref[AFTER - 2, :, cols]) * dot(b, enter_ref[STATE:, cols])
        g_out[:, cols] = (g_ref[:, :, cols].reshape(rows, GROUP) + g_off).astype(BF16)


def finish(b, c, y_a, y_b, g_local, enter, scales, spread_four):
    pieces = scales.shape[0]
    out = jax.ShapeDtypeStruct((pieces * PIECE, WIDTH), BF16)
    square = pl.BlockSpec((RUN, PIECE, PIECE), lambda k: (k, 0, 0))
    half = pl.BlockSpec((RUN, PIECE, HALF), lambda k: (k, 0, 0))
    wide = pl.BlockSpec((RUN, PIECE, WIDTH), lambda k: (k, 0, 0))
    return pl.pallas_call(
        finish_kernel,
        grid=(pieces // RUN,),
        in_specs=[
            square,
            square,
            half,
            half,
            wide,
            pl.BlockSpec((2 * STATE, WIDTH), lambda k: (0, 0)),
            square,
            pl.BlockSpec((2, PIECE, WIDTH), lambda k: (1, 0, 0)),
        ],
        out_specs=[pl.BlockSpec((RUN * PIECE, WIDTH), lambda k: (k, 0))] * 2,
        out_shape=[out, out],
        compiler_params=params(),
        name="finish",
    )(b, c, y_a, y_b, g_local, enter, scales, spread_four)


def ranks(dest):
    owner = dest // OWNERS
    here = lax.broadcasted_iota(jnp.int32, (OWNERS, OWNERS), 0)
    other = lax.broadcasted_iota(jnp.int32, (OWNERS, OWNERS), 1)
    same = (owner[..., None, :] == owner[..., :, None]) & (other < here)
    return jnp.sum(same.astype(jnp.int32), axis=-1)


def to_owners(value):
    return lax.all_to_all(value, "ctx", split_axis=0, concat_axis=0, tiled=True)


def body(
    x_rows, b_rows, c_rows, dt_rows, destination, doc_start, a_log, dt_bias, d_skip, cotangent
):
    head = lax.axis_index("head")
    me = lax.axis_index("ctx")
    dest_heads = jnp.stack([partner(head, s) for s in SHIFTS] + [head]).astype(jnp.int32)
    origin = jnp.stack([source(head, s) for s in SHIFTS] + [head]).astype(jnp.int32)
    send_slot = destination // OWNERS * 2 + ranks(destination)

    small = gather_small(b_rows, c_rows, dt_rows)
    small = lax.all_to_all(small, "head", split_axis=0, concat_axis=0, tiled=True)
    cuts = [cut(half, dest_heads, x_rows) for half in range(2)]
    arrived = []
    for half in range(2):
        arrived.append([])
        for shift, piece in zip(SHIFTS, cuts[half]):
            pairs = [(h, partner(h, shift)) for h in range(PEERS)]
            arrived[half].append(lax.ppermute(piece, "head", pairs))
        arrived[half].append(cuts[half][-1])
    small = small.reshape(OWNERS, SMALL_ROWS, STATE)
    small = pack_small(send_slot, destination % OWNERS, small, arrived[0][:EARLY])
    small = to_owners(small)

    pieces = destination.shape[0]
    seg = jnp.cumsum(doc_start.reshape(pieces, PIECE), axis=1).astype(F32)[:, None, :]
    bias, alog = dt_bias.reshape(HEADS, 1), a_log.reshape(HEADS, 1)
    skip = jnp.repeat(d_skip, HEAD_DIM).reshape(1, WIDTH)
    spread_four = spread(4)
    first = [seg, bias, alog, skip, spread_four, cuts[1][0]]
    x_a = pack_x(send_slot, origin, arrived[0], first)
    x_a = to_owners(x_a)

    src = find_source(small)
    b, c, bt, ct, rows, cols, scales, ends, total = decays(src, small, seg, bias, alog)
    local = (rows, cols, scales, ends, spread_four, skip)
    g_state = leaving_gradient(ct, cotangent, scales, spread_four)
    g_local = backward_local(src, b, ct, cotangent, local, g_state)

    x_b = pack_x(send_slot, origin, arrived[1], [g_state])
    x_slots = [x_a, to_owners(hold(x_b, [g_local]))]
    parts = leaving(src, x_slots, bt, scales, spread_four, g_state, total)
    y_a = forward_local(0, src, c, bt, x_slots, local, parts)
    back = (me >= OWNERS // 2).astype(jnp.int32).reshape(1)
    enter = scan_owners(back, to_owners(parts), y_a)
    y_b = forward_local(1, src, c, bt, x_slots, local, enter)
    enter = to_owners(enter).reshape(2 * STATE, WIDTH)
    return tuple(finish(b, c, y_a, y_b, g_local, enter, scales, spread_four))


def solution(mesh):
    in_specs = (
        P(("ctx", "head"), None),
        P(("ctx", "head"), None),
        P(("ctx", "head"), None),
        P(("ctx", "head"), None),
        P("ctx"),
        P("ctx"),
        P("head"),
        P("head"),
        P("head"),
        P("ctx", "head"),
    )
    out_specs = (P("ctx", "head"), P("ctx", "head"))
    return jax.shard_map(body, mesh=mesh, in_specs=in_specs, out_specs=out_specs, check_vma=False)
```
